32 devices in a mesh: member: 2 (over core), tile: 16 (over z, y, x).
Axes of the slice: x: 2, y: 2, z: 4, core: 2. Of those that a mesh axis runs over, the one named last changes fastest.
Arguments:
- member_predictions: bfloat16 [4, 80, 768, 1536], P(None, 'member', 'tile'), may hold values from -5 to 13
- meridional_operator: float32 [384, 128], replicated, may hold values from -0.3125 to 0.3125
- zonal_operator: float32 [256, 48], P('tile'), may hold values from -0.875 to 0.875
Outputs:
- coarse_anomalies: float32 [4, 80, 512, 256], P(None, None, 'tile', 'member')
The draws below stay inside these ranges and needn't reach their ends.
All inputs are finite; a program needn't handle non-finite values.
Results may differ from the reference program's by a relative error of at most 0.0003.
Values sent between devices are 32-bit elements; how exact they have to be, the bound alone decides.
A program may use at most 128 MiB of HBM per device.

```python
import math
import jax
import jax.numpy as jnp
from jax import lax

M = 80
LEV = 4
LON_DEV = 48
NY = 1536
LB = 384
LBC = 128
NX = 768
NXC = 256


def draw_member_predictions(key, part):
    key = jax.random.fold_in(key, 11)
    key_back, key_pert = jax.random.split(key, 2)
    background = jax.random.uniform(key_back, (LEV, 1, NX, NY), jnp.float32, 2.0, 6.0)
    perturbation = jnp.clip(jax.random.normal(key_pert, (LEV, M, NX, NY), jnp.float32), -5.0, 5.0)
    return (background + perturbation).astype(jnp.bfloat16)


def shard_levels(stream_key, dims, pieces, low, high):
    loudness, own = 1.0, jax.random.fold_in(stream_key, 6)
    for axis_at, shards_of in pieces:
        heights = jnp.exp(jax.random.uniform(jax.random.fold_in(own, axis_at), (shards_of,), jnp.float32, low / len(pieces), high / len(pieces)))
        loudness = loudness * jnp.repeat(heights, dims[axis_at] // shards_of).reshape([-1 if axis == axis_at else 1 for axis in range(len(dims))])
    return loudness


def centred(stream_key, dims, scale, reach, cuts=(), kind=jnp.bfloat16):
    array = jax.random.normal(stream_key, dims, jnp.float32) * scale
    if len(cuts) > 0:
        array = shard_levels(stream_key, dims, cuts, -0.22, 0.18) * array
    return jnp.clip(array, min=-reach, max=reach).astype(kind)


def setup_inputs(seed: int = 0) -> dict:
    splits = jax.random.split(jax.random.key(seed), 4)
    member_predictions = draw_member_predictions(jax.random.fold_in(splits[3], 71), 0)
    meridional_operator = centred(splits[1], (LB, LBC), LB ** -0.5, 0.3125, (), jnp.float32)
    zonal_operator = centred(splits[2], (NXC, LON_DEV), LON_DEV ** -0.5, 0.875, ((0, 16),), jnp.float32)
    return dict(member_predictions=member_predictions, meridional_operator=meridional_operator, zonal_operator=zonal_operator)


def restrict_one(field, meridional_operator, zonal_operator):
    latitude_bands = field.reshape(NX, NY // LB, LB)
    across = jnp.einsum('xbj,jk->xbk', latitude_bands, meridional_operator, precision=lax.Precision.HIGHEST)
    across = across.reshape(NX // LON_DEV, LON_DEV, NY // 3)
    lon_tiled = zonal_operator.reshape(NX // LON_DEV, LON_DEV // 3, LON_DEV)
    result = jnp.einsum('tcx,txi->itc', lon_tiled, across, precision=lax.Precision.HIGHEST)
    return result.reshape(NY // 3, NX // 3)

def one_layer_slice(stacked_layer_states, meridional_operator, zonal_operator):

    def running_total(total, member_field):
        return (total + member_field.astype(jnp.float32), None)
    total, _ = lax.scan(running_total, jnp.zeros((NX, NY), jnp.float32), stacked_layer_states)
    ens_mean = total / M
    scale = 1.0 / math.sqrt(M - 1)

    def per_member(member_field):
        anomaly = (member_field.astype(jnp.float32) - ens_mean) * scale
        return restrict_one(anomaly, meridional_operator, zonal_operator)
    return lax.map(per_member, stacked_layer_states)

def reference(member_predictions, meridional_operator, zonal_operator):
    return lax.map(lambda stacked_layer_states: one_layer_slice(stacked_layer_states, meridional_operator, zonal_operator), member_predictions)
```

```python
import functools
import math

import jax
import jax.numpy as jnp
from jax import lax
from jax.experimental import pallas as pl
from jax.experimental.pallas import tpu as pltpu
from jax.sharding import PartitionSpec as P

MESH = pl.DeviceIdType.MESH
PACK = 8
DEPTH = 3


def two_parts(value):
    high = value.astype(jnp.bfloat16)
    low = (value - high.astype(jnp.float32)).astype(jnp.bfloat16)
    return high, low


def three_parts(value):
    high = value.astype(jnp.bfloat16)
    rest = value - high.astype(jnp.float32)
    middle = rest.astype(jnp.bfloat16)
    low = (rest - middle.astype(jnp.float32)).astype(jnp.bfloat16)
    return high, middle, low


def block_diagonal(part, width):
    coarse = part.shape[0]
    row = lax.broadcasted_iota(jnp.int32, (width, PACK * width), 0)
    col = lax.broadcasted_iota(jnp.int32, (width, PACK * width), 1)
    spread = col == row
    for f in range(1, PACK):
        spread = spread | (col == row + f * width)
    spread = jnp.where(spread, 1.0, 0.0).astype(jnp.bfloat16)
    wide = jnp.dot(part, spread, preferred_element_type=jnp.float32)
    tall = jnp.concatenate([wide] * PACK, axis=0)
    row = lax.broadcasted_iota(jnp.int32, tall.shape, 0)
    col = lax.broadcasted_iota(jnp.int32, tall.shape, 1)
    keep = None
    for f in range(PACK):
        here = (row >= f * coarse) & (row < (f + 1) * coarse) & (col >= f * width) & (col < (f + 1) * width)
        keep = here if keep is None else keep | here
    return jnp.where(keep, tall, 0.0).astype(jnp.bfloat16)


def exchange_kernel(
    members, tiles, x_ref, mer_ref, zon_ref, got_ref, xbuf, zon2, mer2, sendbuf, x_sem, send_sem, recv_sem, own_sem
):
    levels, local, width, fine = x_ref.shape
    block, per_block = mer_ref.shape
    groups, rows, lanes = sendbuf.shape[1:]
    per = PACK // levels
    spread = tiles // members
    half = tiles // 2
    me = lax.axis_index("member")
    tile = lax.axis_index("tile")
    target = tile // spread
    slot_there = me * spread + lax.rem(tile, spread)
    stays = target == me

    barrier = pltpu.get_barrier_semaphore()
    for h in range(members):
        for s in range(spread):
            source = me * spread + s

            @pl.when(jnp.logical_not((h == me) & (source == tile)))
            def _():
                pl.semaphore_signal(barrier, inc=1, device_id=(h, source), device_id_type=MESH)

    def fetch(g, slot):
        return pltpu.make_async_copy(x_ref.at[:, pl.ds(g * per, per)], xbuf.at[slot], x_sem.at[slot])

    for g in range(min(DEPTH, groups)):
        fetch(g, g).start()

    zon_high, zon_low = two_parts(zon_ref[...])
    zon2[: PACK * zon_ref.shape[0]] = block_diagonal(zon_high, width)
    zon2[PACK * zon_ref.shape[0] :] = block_diagonal(zon_low, width)
    mer_high, mer_low = two_parts(mer_ref[...].T)
    mer2[:per_block] = mer_high
    mer2[per_block:] = mer_low

    def destination(k):
        side = tile // half
        side = 1 - side if k < half else side
        return side * half + lax.rem(lax.rem(tile, half) + k, half)

    def remote(k, g):
        there = destination(k)
        return pltpu.make_async_remote_copy(
            src_ref=sendbuf.at[there, g],
            dst_ref=got_ref.at[slot_there, g],
            send_sem=send_sem.at[k],
            recv_sem=recv_sem.at[slot_there],
            device_id=(target, there),
            device_id_type=MESH,
        )

    def step(g, _):
        slot = lax.rem(g, DEPTH)
        fetch(g, slot).wait()
        fields = xbuf[slot].reshape(PACK * width, fine)
        across = jnp.dot(zon2[...], fields, preferred_element_type=jnp.float32)
        across = across[lanes:] + across[:lanes]
        for b in range(fine // block):
            high, middle, low = three_parts(across[:, b * block : (b + 1) * block])
            parts = jnp.concatenate([high, middle, low], axis=0)
            out = lax.dot_general(
                mer2[...], parts, (((1,), (1,)), ((), ())), preferred_element_type=jnp.float32
            )
            top, bottom = out[:per_block], out[per_block:]
            total = top[:, 2 * lanes :] + bottom[:, lanes : 2 * lanes]
            total = total + top[:, lanes : 2 * lanes] + bottom[:, :lanes]
            total = total + top[:, :lanes]
            for q in range(per_block // rows):
                sendbuf[b * (per_block // rows) + q, g] = total[q * rows : (q + 1) * rows]

        @pl.when(g + DEPTH < groups)
        def _():
            fetch(g + DEPTH, slot).start()

        @pl.when(g == 0)
        def _():
            pl.semaphore_wait(barrier, tiles - jnp.where(stays, 1, 0))

        for k in range(tiles):
            if k == half:

                @pl.when(stays)
                def _():
                    pltpu.make_async_copy(sendbuf.at[tile, g], got_ref.at[slot_there, g], own_sem).start()

                @pl.when(jnp.logical_not(stays))
                def _():
                    remote(k, g).start()

            else:
                remote(k, g).start()
        return 0

    lax.fori_loop(0, groups, step, 0)

    def whole(k, slot):
        return pltpu.make_async_remote_copy(
            src_ref=sendbuf.at[destination(k)],
            dst_ref=got_ref.at[slot],
            send_sem=send_sem.at[k],
            recv_sem=recv_sem.at[slot],
            device_id=(target, destination(k)),
            device_id_type=MESH,
        )

    for k in range(tiles):
        if k == half:

            @pl.when(stays)
            def _():
                pltpu.make_async_copy(sendbuf.at[tile], got_ref.at[slot_there], own_sem).wait()

            @pl.when(jnp.logical_not(stays))
            def _():
                whole(k, slot_there).wait_send()

        else:
            whole(k, slot_there).wait_send()
    for slot in range(tiles):

        @pl.when(jnp.logical_not(stays & (slot_there == slot)))
        def _():
            whole(0, slot).wait_recv()


def swap_pieces(blocks, piece):
    lanes = blocks[0].shape[-1]
    lane = lax.broadcasted_iota(jnp.int32, blocks[0].shape, blocks[0].ndim - 1)
    axis = blocks[0].ndim - 1
    blocks = list(blocks)
    d = PACK // 2
    while d >= 1:
        shift = d * piece
        upper = (lane & shift) != 0
        for s in range(PACK):
            if s & d:
                continue
            a, b = blocks[s], blocks[s + d]
            if 2 * shift == lanes:
                both = pltpu.roll(jnp.where(upper, a, b), shift, axis)
                blocks[s] = jnp.where(upper, both, a)
                blocks[s + d] = jnp.where(upper, b, both)
            else:
                blocks[s] = jnp.where(upper, pltpu.roll(b, shift, axis), a)
                blocks[s + d] = jnp.where(upper, b, pltpu.roll(a, lanes - shift, axis))
        d //= 2
    return blocks


def anomaly_kernel(members, tiles, got_ref, out_ref):
    levels, count, rows, _ = out_ref.shape
    groups = got_ref.shape[1]
    lanes = got_ref.shape[3]
    per = PACK // levels
    local = count // members
    spread = tiles // members
    scale = 1.0 / math.sqrt(count - 1)
    for side in range(spread // PACK):
        columns = slice(side * lanes, (side + 1) * lanes)
        sums = tuple(jnp.zeros((rows, lanes), jnp.float32) for _ in range(levels))
        for h in range(members):
            base = h * spread + side * PACK

            def gather(g, sums, base=base, h=h):
                fields = swap_pieces([got_ref[base + s, g] for s in range(PACK)], lanes // PACK)
                sums = list(sums)
                for f in range(PACK):
                    level, m = divmod(f, per)
                    out_ref[level, h * local + g * per + m, :, columns] = fields[f]
                    sums[level] = sums[level] + fields[f]
                return tuple(sums)

            sums = lax.fori_loop(0, groups, gather, sums, unroll=2)
        means = [total / count for total in sums]

        def center(m, _):
            for level in range(levels):
                out_ref[level, m, :, columns] = (out_ref[level, m, :, columns] - means[level]) * scale
            return 0

        lax.fori_loop(0, count, center, 0, unroll=4)


def body(members, tiles, x, meridional, zonal):
    levels, local, width, fine = x.shape
    block, per_block = meridional.shape
    coarse = zonal.shape[0]
    lanes = PACK * coarse
    groups = levels * local // PACK
    rows = fine // block * per_block // tiles
    spread = tiles // members
    assert PACK % levels == 0 and local % (PACK // levels) == 0 and spread % PACK == 0 and per_block % rows == 0
    vmem = pl.BlockSpec(memory_space=pltpu.VMEM)
    anywhere = pl.BlockSpec(memory_space=pl.ANY)
    got = pl.pallas_call(
        functools.partial(exchange_kernel, members, tiles),
        out_shape=jax.ShapeDtypeStruct((tiles, groups, rows, lanes), jnp.float32),
        in_specs=[anywhere, vmem, vmem],
        out_specs=anywhere,
        scratch_shapes=[
            pltpu.VMEM((DEPTH, levels, PACK // levels, width, fine), jnp.bfloat16),
            pltpu.VMEM((2 * lanes, PACK * width), jnp.bfloat16),
            pltpu.VMEM((2 * per_block, block), jnp.bfloat16),
            pltpu.VMEM((tiles, groups, rows, lanes), jnp.float32),
            pltpu.SemaphoreType.DMA((DEPTH,)),
            pltpu.SemaphoreType.DMA((tiles,)),
            pltpu.SemaphoreType.DMA((tiles,)),
            pltpu.SemaphoreType.DMA,
        ],
        compiler_params=pltpu.CompilerParams(
            collective_id=0, has_side_effects=True, vmem_limit_bytes=40 * 1024 * 1024
        ),
        name="restrict_exchange",
    )(x, meridional, zonal)
    height = 8 if rows % 8 == 0 else rows
    return pl.pallas_call(
        functools.partial(anomaly_kernel, members, tiles),
        grid=(rows // height,),
        out_shape=jax.ShapeDtypeStruct((levels, local * members, rows, spread * coarse), jnp.float32),
        in_specs=[pl.BlockSpec((tiles, groups, height, lanes), lambda i: (0, 0, i, 0))],
        out_specs=pl.BlockSpec((levels, local * members, height, spread * coarse), lambda i: (0, 0, i, 0)),
        compiler_params=pltpu.CompilerParams(vmem_limit_bytes=40 * 1024 * 1024),
        name="center_scale",
    )(got)


def solution(mesh):
    members, tiles = mesh.shape["member"], mesh.shape["tile"]
    return jax.shard_map(
        functools.partial(body, members, tiles),
        mesh=mesh,
        in_specs=(P(None, "member", "tile", None), P(), P("tile", None)),
        out_specs=P(None, None, "tile", "member"),
        check_vma=False,
    )
```

```python
import functools
import math

import jax
import jax.numpy as jnp
from jax import lax
from jax.experimental import pallas as pl
from jax.experimental.pallas import tpu as pltpu
from jax.sharding import PartitionSpec as P

MESH = pl.DeviceIdType.MESH
PACK = 8
DEPTH = 3


def two_parts(value):
    high = value.astype(jnp.bfloat16)
    low = (value - high.astype(jnp.float32)).astype(jnp.bfloat16)
    return high, low


def three_parts(value):
    high = value.astype(jnp.bfloat16)
    rest = value - high.astype(jnp.float32)
    middle = rest.astype(jnp.bfloat16)
    low = (rest - middle.astype(jnp.float32)).astype(jnp.bfloat16)
    return high, middle, low


def block_diagonal(part, width):
    coarse = part.shape[0]
    row = lax.broadcasted_iota(jnp.int32, (width, PACK * width), 0)
    col = lax.broadcasted_iota(jnp.int32, (width, PACK * width), 1)
    spread = col == row
    for f in range(1, PACK):
        spread = spread | (col == row + f * width)
    spread = jnp.where(spread, 1.0, 0.0).astype(jnp.bfloat16)
    wide = jnp.dot(part, spread, preferred_element_type=jnp.float32)
    tall = jnp.concatenate([wide] * PACK, axis=0)
    row = lax.broadcasted_iota(jnp.int32, tall.shape, 0)
    col = lax.broadcasted_iota(jnp.int32, tall.shape, 1)
    keep = None
    for f in range(PACK):
        here = (row >= f * coarse) & (row < (f + 1) * coarse) & (col >= f * width) & (col < (f + 1) * width)
        keep = here if keep is None else keep | here
    return jnp.where(keep, tall, 0.0).astype(jnp.bfloat16)


def swap_pieces(blocks, piece):
    lanes = blocks[0].shape[-1]
    lane = lax.broadcasted_iota(jnp.int32, blocks[0].shape, blocks[0].ndim - 1)
    axis = blocks[0].ndim - 1
    blocks = list(blocks)
    d = PACK // 2
    while d >= 1:
        shift = d * piece
        upper = (lane & shift) != 0
        for s in range(PACK):
            if s & d:
                continue
            a, b = blocks[s], blocks[s + d]
            if 2 * shift == lanes:
                both = pltpu.roll(jnp.where(upper, a, b), shift, axis)
                blocks[s] = jnp.where(upper, both, a)
                blocks[s + d] = jnp.where(upper, b, both)
            else:
                blocks[s] = jnp.where(upper, pltpu.roll(b, shift, axis), a)
                blocks[s + d] = jnp.where(upper, b, pltpu.roll(a, lanes - shift, axis))
        d //= 2
    return blocks


def exchange_kernel(
    members,
    tiles,
    x_ref,
    mer_hbm,
    zon_hbm,
    raw_ref,
    mean_ref,
    xbuf,
    mer_ref,
    zon_ref,
    zon2,
    mer2,
    sendbuf,
    got_ref,
    rawbuf,
    sumbuf,
    x_sem,
    op_sem,
    send_sem,
    recv_sem,
    own_sem,
    out_sem,
):
    levels, local, width, fine = x_ref.shape
    block, per_block = mer_ref.shape
    groups, rows, lanes = sendbuf.shape[1:]
    per = PACK // levels
    spread = tiles // members
    half = tiles // 2
    me = lax.axis_index("member")
    tile = lax.axis_index("tile")
    target = tile // spread
    slot_there = me * spread + lax.rem(tile, spread)
    stays = target == me

    barrier = pltpu.get_barrier_semaphore()
    for h in range(members):
        for s in range(spread):
            source = me * spread + s

            @pl.when(jnp.logical_not((h == me) & (source == tile)))
            def _():
                pl.semaphore_signal(barrier, inc=1, device_id=(h, source), device_id_type=MESH)

    def fetch(g, slot):
        return pltpu.make_async_copy(x_ref.at[:, pl.ds(g * per, per)], xbuf.at[slot], x_sem.at[slot])

    operators = [
        pltpu.make_async_copy(zon_hbm, zon_ref, op_sem.at[0]),
        pltpu.make_async_copy(mer_hbm, mer_ref, op_sem.at[1]),
    ]
    for copy in operators:
        copy.start()
    for g in range(min(DEPTH, groups)):
        fetch(g, g).start()
    for copy in operators:
        copy.wait()

    zon_high, zon_low = two_parts(zon_ref[...])
    zon2[: PACK * zon_ref.shape[0]] = block_diagonal(zon_high, width)
    zon2[PACK * zon_ref.shape[0] :] = block_diagonal(zon_low, width)
    mer_high, mer_low = two_parts(mer_ref[...].T)
    mer2[:per_block] = mer_high
    mer2[per_block:] = mer_low

    def destination(k):
        side = tile // half
        side = 1 - side if k < half else side
        return side * half + lax.rem(lax.rem(tile, half) + k, half)

    def remote(k, g):
        there = destination(k)
        return pltpu.make_async_remote_copy(
            src_ref=sendbuf.at[there, g],
            dst_ref=got_ref.at[slot_there, g],
            send_sem=send_sem.at[k],
            recv_sem=recv_sem.at[slot_there, g],
            device_id=(target, there),
            device_id_type=MESH,
        )

    def step(g, _):
        slot = lax.rem(g, DEPTH)
        fetch(g, slot).wait()
        fields = xbuf[slot].reshape(PACK * width, fine)
        across = jnp.dot(zon2[...], fields, preferred_element_type=jnp.float32)
        across = across[lanes:] + across[:lanes]
        for b in range(fine // block):
            high, middle, low = three_parts(across[:, b * block : (b + 1) * block])
            parts = jnp.concatenate([high, middle, low], axis=0)
            out = lax.dot_general(
                mer2[...], parts, (((1,), (1,)), ((), ())), preferred_element_type=jnp.float32
            )
            top, bottom = out[:per_block], out[per_block:]
            total = top[:, 2 * lanes :] + bottom[:, lanes : 2 * lanes]
            total = total + top[:, lanes : 2 * lanes] + bottom[:, :lanes]
            total = total + top[:, :lanes]
            for q in range(per_block // rows):
                sendbuf[b * (per_block // rows) + q, g] = total[q * rows : (q + 1) * rows]

        @pl.when(g + DEPTH < groups)
        def _():
            fetch(g + DEPTH, slot).start()

        @pl.when(g == 0)
        def _():
            pl.semaphore_wait(barrier, tiles - jnp.where(stays, 1, 0))

        for k in range(tiles):
            if k == half:

                @pl.when(stays)
                def _():
                    pltpu.make_async_copy(sendbuf.at[tile, g], got_ref.at[slot_there, g], own_sem).start()

                @pl.when(jnp.logical_not(stays))
                def _():
                    remote(k, g).start()

            else:
                remote(k, g).start()
        return 0

    lax.fori_loop(0, groups, step, 0)

    @pl.when(stays)
    def _():
        pltpu.make_async_copy(sendbuf.at[tile], got_ref.at[slot_there], own_sem).wait()

    sumbuf[...] = jnp.zeros_like(sumbuf)
    count = members * local

    def arrival(g, _):
        for slot in range(tiles):

            @pl.when(jnp.logical_not(stays & (slot_there == slot)))
            def _():
                pltpu.make_async_remote_copy(
                    src_ref=sendbuf.at[0, g],
                    dst_ref=got_ref.at[slot, g],
                    send_sem=send_sem.at[0],
                    recv_sem=recv_sem.at[slot, g],
                    device_id=(target, destination(0)),
                    device_id_type=MESH,
                ).wait_recv()

        for h in range(members):
            for side in range(spread // PACK):
                base = h * spread + side * PACK
                columns = slice(side * lanes, (side + 1) * lanes)
                fields = swap_pieces([got_ref[base + s, g] for s in range(PACK)], lanes // PACK)
                for f in range(PACK):
                    rawbuf[f // per, h * local + g * per + f % per, :, columns] = fields[f]
                for level in range(levels):
                    total = fields[level * per]
                    for m in range(1, per):
                        total = total + fields[level * per + m]
                    sumbuf[level, :, columns] += total
            done = pl.ds(h * local + g * per, per)
            pltpu.make_async_copy(rawbuf.at[:, done], raw_ref.at[:, done], out_sem.at[0]).start()
        return 0

    lax.fori_loop(0, groups, arrival, 0)
    sumbuf[...] = sumbuf[...] / count
    mean = pltpu.make_async_copy(sumbuf, mean_ref, out_sem.at[1])
    mean.start()

    def whole(k):
        return pltpu.make_async_remote_copy(
            src_ref=sendbuf.at[destination(k)],
            dst_ref=got_ref.at[slot_there],
            send_sem=send_sem.at[k],
            recv_sem=recv_sem.at[slot_there, 0],
            device_id=(target, destination(k)),
            device_id_type=MESH,
        )

    for k in range(tiles):
        if k == half:

            @pl.when(jnp.logical_not(stays))
            def _():
                whole(k).wait_send()

        else:
            whole(k).wait_send()
    pltpu.make_async_copy(rawbuf, raw_ref, out_sem.at[0]).wait()
    mean.wait()


def body(members, tiles, x, meridional, zonal):
    levels, local, width, fine = x.shape
    block, per_block = meridional.shape
    coarse = zonal.shape[0]
    lanes = PACK * coarse
    groups = levels * local // PACK
    rows = fine // block * per_block // tiles
    spread = tiles // members
    assert PACK % levels == 0 and local % (PACK // levels) == 0 and spread % PACK == 0 and per_block % rows == 0
    anywhere = pl.BlockSpec(memory_space=pl.ANY)
    count = local * members
    columns = spread * coarse
    raw, mean = pl.pallas_call(
        functools.partial(exchange_kernel, members, tiles),
        out_shape=[
            jax.ShapeDtypeStruct((levels, count, rows, columns), jnp.float32),
            jax.ShapeDtypeStruct((levels, rows, columns), jnp.float32),
        ],
        in_specs=[pl.BlockSpec(memory_space=pltpu.HBM)] * 3,
        out_specs=[anywhere] * 2,
        scratch_shapes=[
            pltpu.VMEM((DEPTH, levels, PACK // levels, width, fine), jnp.bfloat16),
            pltpu.VMEM(meridional.shape, jnp.float32),
            pltpu.VMEM(zonal.shape, jnp.float32),
            pltpu.VMEM((2 * lanes, PACK * width), jnp.bfloat16),
            pltpu.VMEM((2 * per_block, block), jnp.bfloat16),
            pltpu.VMEM((tiles, groups, rows, lanes), jnp.float32),
            pltpu.VMEM((tiles, groups, rows, lanes), jnp.float32),
            pltpu.VMEM((levels, count, rows, columns), jnp.float32),
            pltpu.VMEM((levels, rows, columns), jnp.float32),
            pltpu.SemaphoreType.DMA((DEPTH,)),
            pltpu.SemaphoreType.DMA((2,)),
            pltpu.SemaphoreType.DMA((tiles,)),
            pltpu.SemaphoreType.DMA((tiles, groups)),
            pltpu.SemaphoreType.DMA,
            pltpu.SemaphoreType.DMA((2,)),
        ],
        compiler_params=pltpu.CompilerParams(
            collective_id=0, has_side_effects=True, vmem_limit_bytes=40 * 1024 * 1024
        ),
        name="restrict_exchange",
    )(x, meridional, zonal)
    return (raw - mean[:, None]) * (1.0 / math.sqrt(count - 1))


def solution(mesh):
    members, tiles = mesh.shape["member"], mesh.shape["tile"]
    return jax.shard_map(
        functools.partial(body, members, tiles),
        mesh=mesh,
        in_specs=(P(None, "member", "tile", None), P(), P("tile", None)),
        out_specs=P(None, None, "tile", "member"),
        check_vma=False,
    )
```

```python
import functools
import math

import jax
import jax.numpy as jnp
from jax import lax
from jax.experimental import pallas as pl
from jax.experimental.pallas import tpu as pltpu
from jax.sharding import PartitionSpec as P

MESH = pl.DeviceIdType.MESH
PACK = 8
DEPTH = 3


def two_parts(value):
    high = value.astype(jnp.bfloat16)
    low = (value - high.astype(jnp.float32)).astype(jnp.bfloat16)
    return high, low


def three_parts(value):
    high = value.astype(jnp.bfloat16)
    rest = value - high.astype(jnp.float32)
    middle = rest.astype(jnp.bfloat16)
    low = (rest - middle.astype(jnp.float32)).astype(jnp.bfloat16)
    return high, middle, low


def piece_index(shape, dimension, size):
    at = lax.broadcasted_iota(jnp.int32, shape, dimension)
    piece = jnp.zeros(shape, jnp.int32)
    for f in range(1, PACK):
        piece = piece + jnp.where(at >= f * size, 1, 0)
    return piece


def block_diagonal(part, width):
    coarse = part.shape[0]
    row_piece = piece_index((PACK * coarse, 1), 0, coarse)
    col_piece = piece_index((1, PACK * width), 1, width)
    within = lax.broadcasted_iota(jnp.int32, (1, PACK * width), 1) - col_piece * width
    spread = lax.broadcasted_iota(jnp.int32, (width, PACK * width), 0) == within
    spread = jnp.where(spread, 1.0, 0.0).astype(jnp.bfloat16)
    wide = jnp.dot(part, spread, preferred_element_type=jnp.float32)
    tall = jnp.concatenate([wide] * PACK, axis=0)
    return jnp.where(row_piece == col_piece, tall, 0.0).astype(jnp.bfloat16)


def swap_pieces(blocks, piece):
    lanes = blocks[0].shape[-1]
    lane = lax.broadcasted_iota(jnp.int32, blocks[0].shape, blocks[0].ndim - 1)
    axis = blocks[0].ndim - 1
    blocks = list(blocks)
    d = PACK // 2
    while d >= 1:
        shift = d * piece
        upper = (lane & shift) != 0
        for s in range(PACK):
            if s & d:
                continue
            a, b = blocks[s], blocks[s + d]
            if 2 * shift == lanes:
                both = pltpu.roll(jnp.where(upper, a, b), shift, axis)
                blocks[s] = jnp.where(upper, both, a)
                blocks[s + d] = jnp.where(upper, b, both)
            else:
                blocks[s] = jnp.where(upper, pltpu.roll(b, shift, axis), a)
                blocks[s + d] = jnp.where(upper, b, pltpu.roll(a, lanes - shift, axis))
        d //= 2
    return blocks


def exchange_kernel(
    members,
    tiles,
    x_ref,
    mer_hbm,
    zon_hbm,
    raw_ref,
    mean_ref,
    xbuf,
    mer_ref,
    zon_ref,
    zon2,
    mer2,
    across_ref,
    sendbuf,
    got_ref,
    x_sem,
    op_sem,
    send_sem,
    recv_sem,
    own_sem,
):
    levels, local, width, fine = x_ref.shape
    block, per_block = mer_ref.shape
    groups, rows, lanes = sendbuf.shape[1:]
    per = PACK // levels
    spread = tiles // members
    bands = fine // block
    tiles_per_band = tiles // bands
    count = members * local
    me = lax.axis_index("member")
    tile = lax.axis_index("tile")
    target = tile // spread
    slot_there = me * spread + lax.rem(tile, spread)
    stays = target == me
    side = tile // (tiles // 2)

    def fetch(g, slot):
        return pltpu.make_async_copy(x_ref.at[:, pl.ds(g * per, per)], xbuf.at[slot], x_sem.at[slot])

    operators = [
        pltpu.make_async_copy(zon_hbm, zon_ref, op_sem.at[0]),
        pltpu.make_async_copy(mer_hbm, mer_ref, op_sem.at[1]),
    ]
    for copy in operators:
        copy.start()
    fetch(0, 0).start()

    barrier = pltpu.get_barrier_semaphore()
    for h in range(members):
        for s in range(spread):
            source = me * spread + s

            @pl.when(jnp.logical_not((h == me) & (source == tile)))
            def _():
                pl.semaphore_signal(barrier, inc=1, device_id=(h, source), device_id_type=MESH)

    for copy in operators:
        copy.wait()
    zon_high, zon_low = two_parts(zon_ref[...])
    zon2[: PACK * zon_ref.shape[0]] = block_diagonal(zon_high, width)
    zon2[PACK * zon_ref.shape[0] :] = block_diagonal(zon_low, width)
    mer_high, mer_low = two_parts(mer_ref[...].T)
    mer2[:per_block] = mer_high
    mer2[per_block:] = mer_low
    for g in range(1, min(DEPTH, groups)):
        fetch(g, g).start()

    def remote(there, g):
        return pltpu.make_async_remote_copy(
            src_ref=sendbuf.at[there, g],
            dst_ref=got_ref.at[slot_there, g],
            send_sem=send_sem.at[there],
            recv_sem=recv_sem.at[slot_there, g],
            device_id=(target, there),
            device_id_type=MESH,
        )

    def step(g, _):
        slot = lax.rem(g, DEPTH)
        fetch(g, slot).wait()
        fields = xbuf[slot].reshape(PACK * width, fine)
        across = jnp.dot(zon2[...], fields, preferred_element_type=jnp.float32)
        across_ref[...] = across[lanes:] + across[:lanes]
        for j in range(bands):
            band = lax.rem((1 - side) * (bands // 2) + j, bands)
            first = band * tiles_per_band
            piece = across_ref[:, pl.ds(pl.multiple_of(band * block, block), block)]
            high, middle, low = three_parts(piece)
            parts = jnp.concatenate([high, middle, low], axis=0)
            out = lax.dot_general(
                mer2[...], parts, (((1,), (1,)), ((), ())), preferred_element_type=jnp.float32
            )
            top, bottom = out[:per_block], out[per_block:]
            total = top[:, 2 * lanes :] + bottom[:, lanes : 2 * lanes]
            total = total + top[:, lanes : 2 * lanes] + bottom[:, :lanes]
            total = total + top[:, :lanes]
            for q in range(tiles_per_band):
                sendbuf[first + q, g] = total[q * rows : (q + 1) * rows]

            if j == 0:

                @pl.when(g == 0)
                def _():
                    pl.semaphore_wait(barrier, tiles - jnp.where(stays, 1, 0))

            for q in range(tiles_per_band):
                there = first + lax.rem(tile + q, tiles_per_band)
                if q == 0 and j >= bands // 2:
                    own = stays & (there == tile)

                    @pl.when(own)
                    def _():
                        pltpu.make_async_copy(sendbuf.at[tile, g], got_ref.at[slot_there, g], own_sem).start()

                    @pl.when(jnp.logical_not(own))
                    def _():
                        remote(there, g).start()

                else:
                    remote(there, g).start()

        @pl.when(g + DEPTH < groups)
        def _():
            fetch(g + DEPTH, slot).start()

        return 0

    lax.fori_loop(0, groups, step, 0)

    @pl.when(stays)
    def _():
        pltpu.make_async_copy(sendbuf.at[tile], got_ref.at[slot_there], own_sem).wait()

    mean_ref[...] = jnp.zeros_like(mean_ref)

    def arrival(g, _):
        for h in range(members):
            for slot in range(h * spread, (h + 1) * spread):

                @pl.when(jnp.logical_not(stays & (slot_there == slot)))
                def _():
                    pltpu.make_async_remote_copy(
                        src_ref=sendbuf.at[0, g],
                        dst_ref=got_ref.at[slot, g],
                        send_sem=send_sem.at[0],
                        recv_sem=recv_sem.at[slot, g],
                        device_id=(target, 0),
                        device_id_type=MESH,
                    ).wait_recv()

            for part in range(spread // PACK):
                base = h * spread + part * PACK
                columns = slice(part * lanes, (part + 1) * lanes)
                fields = swap_pieces([got_ref[base + s, g] for s in range(PACK)], lanes // PACK)
                for f in range(PACK):
                    raw_ref[f // per, h * local + g * per + f % per, :, columns] = fields[f]
                for level in range(levels):
                    total = fields[level * per]
                    for m in range(1, per):
                        total = total + fields[level * per + m]
                    mean_ref[level, :, columns] += total
        return 0

    lax.fori_loop(0, groups - 1, arrival, 0)
    for there in range(tiles):

        @pl.when(jnp.logical_not(stays & (tile == there)))
        def _():
            pltpu.make_async_remote_copy(
                src_ref=sendbuf.at[there],
                dst_ref=got_ref.at[slot_there],
                send_sem=send_sem.at[there],
                recv_sem=recv_sem.at[slot_there, 0],
                device_id=(target, there),
                device_id_type=MESH,
            ).wait_send()

    lax.fori_loop(groups - 1, groups, arrival, 0)
    mean_ref[...] = mean_ref[...] / count


def center_kernel(chunk, raw_ref, mean_ref, out_ref, outbuf, sem):
    levels, count = raw_ref.shape[:2]
    scale = 1.0 / math.sqrt(count - 1)
    for level in range(levels):
        mean = mean_ref[level]
        for start in range(0, count, chunk):

            def center(m, _, start=start, level=level, mean=mean):
                outbuf[level, start + m] = (raw_ref[level, start + m] - mean) * scale
                return 0

            lax.fori_loop(0, chunk, center, 0, unroll=5)
            at = pl.ds(start, chunk)
            pltpu.make_async_copy(outbuf.at[level, at], out_ref.at[level, at], sem).start()
    pltpu.make_async_copy(outbuf, out_ref, sem).wait()


def body(members, tiles, x, meridional, zonal):
    levels, local, width, fine = x.shape
    block, per_block = meridional.shape
    coarse = zonal.shape[0]
    lanes = PACK * coarse
    groups = levels * local // PACK
    rows = fine // block * per_block // tiles
    spread = tiles // members
    assert PACK % levels == 0 and local % (PACK // levels) == 0 and spread % PACK == 0 and per_block % rows == 0
    assert fine // block % 2 == 0
    anywhere = pl.BlockSpec(memory_space=pl.ANY)
    count = local * members
    columns = spread * coarse
    raw, mean = pl.pallas_call(
        functools.partial(exchange_kernel, members, tiles),
        out_shape=[
            jax.ShapeDtypeStruct((levels, count, rows, columns), jnp.float32),
            jax.ShapeDtypeStruct((levels, rows, columns), jnp.float32),
        ],
        in_specs=[pl.BlockSpec(memory_space=pltpu.HBM)] * 3,
        out_specs=[pl.BlockSpec(memory_space=pltpu.VMEM)] * 2,
        scratch_shapes=[
            pltpu.VMEM((DEPTH, levels, PACK // levels, width, fine), jnp.bfloat16),
            pltpu.VMEM(meridional.shape, jnp.float32),
            pltpu.VMEM(zonal.shape, jnp.float32),
            pltpu.VMEM((2 * lanes, PACK * width), jnp.bfloat16),
            pltpu.VMEM((2 * per_block, block), jnp.bfloat16),
            pltpu.VMEM((lanes, fine), jnp.float32),
            pltpu.VMEM((tiles, groups, rows, lanes), jnp.float32),
            pltpu.VMEM((tiles, groups, rows, lanes), jnp.float32),
            pltpu.SemaphoreType.DMA((DEPTH,)),
            pltpu.SemaphoreType.DMA((2,)),
            pltpu.SemaphoreType.DMA((tiles,)),
            pltpu.SemaphoreType.DMA((tiles, groups)),
            pltpu.SemaphoreType.DMA,
        ],
        compiler_params=pltpu.CompilerParams(
            collective_id=0, has_side_effects=True, vmem_limit_bytes=40 * 1024 * 1024
        ),
        name="restrict_exchange",
    )(x, meridional, zonal)
    return pl.pallas_call(
        functools.partial(center_kernel, 16 if count % 16 == 0 else count),
        out_shape=jax.ShapeDtypeStruct((levels, count, rows, columns), jnp.float32),
        in_specs=[pl.BlockSpec(memory_space=pltpu.VMEM)] * 2,
        out_specs=anywhere,
        scratch_shapes=[
            pltpu.VMEM((levels, count, rows, columns), jnp.float32),
            pltpu.SemaphoreType.DMA,
        ],
        compiler_params=pltpu.CompilerParams(vmem_limit_bytes=16 * 1024 * 1024),
        name="center_scale",
    )(raw, mean)


def solution(mesh):
    members, tiles = mesh.shape["member"], mesh.shape["tile"]
    return jax.shard_map(
        functools.partial(body, members, tiles),
        mesh=mesh,
        in_specs=(P(None, "member", "tile", None), P(), P("tile", None)),
        out_specs=P(None, None, "tile", "member"),
        check_vma=False,
    )
```

```python
import functools
import math

import jax
import jax.numpy as jnp
from jax import lax
from jax.experimental import pallas as pl
from jax.experimental.pallas import tpu as pltpu
from jax.sharding import PartitionSpec as P

MESH = pl.DeviceIdType.MESH
PACK = 8
DEPTH = 3


def two_parts(value):
    high = value.astype(jnp.bfloat16)
    low = (value - high.astype(jnp.float32)).astype(jnp.bfloat16)
    return high, low


def three_parts(value):
    high = value.astype(jnp.bfloat16)
    rest = value - high.astype(jnp.float32)
    middle = rest.astype(jnp.bfloat16)
    low = (rest - middle.astype(jnp.float32)).astype(jnp.bfloat16)
    return high, middle, low


def piece_index(shape, dimension, size):
    at = lax.broadcasted_iota(jnp.int32, shape, dimension)
    piece = jnp.zeros(shape, jnp.int32)
    for f in range(1, PACK):
        piece = piece + jnp.where(at >= f * size, 1, 0)
    return piece


def block_diagonal(part, width):
    coarse = part.shape[0]
    row_piece = piece_index((PACK * coarse, 1), 0, coarse)
    col_piece = piece_index((1, PACK * width), 1, width)
    within = lax.broadcasted_iota(jnp.int32, (1, PACK * width), 1) - col_piece * width
    spread = lax.broadcasted_iota(jnp.int32, (width, PACK * width), 0) == within
    spread = jnp.where(spread, 1.0, 0.0).astype(jnp.bfloat16)
    wide = jnp.dot(part, spread, preferred_element_type=jnp.float32)
    tall = jnp.concatenate([wide] * PACK, axis=0)
    return jnp.where(row_piece == col_piece, tall, 0.0).astype(jnp.bfloat16)


def swap_pieces(blocks, piece):
    lanes = blocks[0].shape[-1]
    lane = lax.broadcasted_iota(jnp.int32, blocks[0].shape, blocks[0].ndim - 1)
    axis = blocks[0].ndim - 1
    blocks = list(blocks)
    d = PACK // 2
    while d >= 1:
        shift = d * piece
        upper = (lane & shift) != 0
        for s in range(PACK):
            if s & d:
                continue
            a, b = blocks[s], blocks[s + d]
            if 2 * shift == lanes:
                both = pltpu.roll(jnp.where(upper, a, b), shift, axis)
                blocks[s] = jnp.where(upper, both, a)
                blocks[s + d] = jnp.where(upper, b, both)
            else:
                blocks[s] = jnp.where(upper, pltpu.roll(b, shift, axis), a)
                blocks[s + d] = jnp.where(upper, b, pltpu.roll(a, lanes - shift, axis))
        d //= 2
    return blocks


def exchange_kernel(
    members,
    tiles,
    block,
    x_ref,
    op_ref,
    raw_ref,
    mean_ref,
    xbuf,
    zon2,
    mer2,
    across_ref,
    sendbuf,
    got_ref,
    first_ref,
    x_sem,
    first_send_sem,
    first_recv_sem,
    short_sem,
    send_sem,
    recv_sem,
    own_sem,
):
    levels, local, width, fine = x_ref.shape
    per_block = op_ref.shape[1]
    groups, rows, lanes = sendbuf.shape[1:]
    per = PACK // levels
    spread = tiles // members
    bands = fine // block
    tiles_per_band = tiles // bands
    count = members * local
    piece = lanes // PACK
    packed = per == 2 and rows % 16 == 0
    me = lax.axis_index("member")
    tile = lax.axis_index("tile")
    target = tile // spread
    slot_there = me * spread + lax.rem(tile, spread)
    stays = target == me
    side = tile // (tiles // 2)

    def fetch(g, slot):
        return pltpu.make_async_copy(x_ref.at[:, pl.ds(g * per, per)], xbuf.at[slot], x_sem.at[slot])

    fetch(0, 0).start()

    barrier = pltpu.get_barrier_semaphore()
    for h in range(members):
        for s in range(spread):
            source = me * spread + s

            @pl.when(jnp.logical_not((h == me) & (source == tile)))
            def _():
                pl.semaphore_signal(barrier, inc=1, device_id=(h, source), device_id_type=MESH)

    @pl.when(me != 0)
    def _():
        pl.semaphore_signal(barrier, inc=1, device_id=(0, tile), device_id_type=MESH)

    zon_high, zon_low = two_parts(op_ref[block : block + piece, :width])
    zon2[:lanes] = block_diagonal(zon_high, width)
    zon2[lanes:] = block_diagonal(zon_low, width)
    mer_high, mer_low = two_parts(op_ref[:block].T)
    mer2[:per_block] = mer_high
    mer2[per_block:] = mer_low
    for g in range(1, min(DEPTH, groups)):
        fetch(g, g).start()

    def remote(there, g, short=False):
        height = pl.ds(0, rows // 2 if short else rows)
        return pltpu.make_async_remote_copy(
            src_ref=sendbuf.at[there, g, height],
            dst_ref=got_ref.at[slot_there, g, height],
            send_sem=(short_sem if isinstance(g, int) else send_sem).at[there],
            recv_sem=recv_sem.at[slot_there, g],
            device_id=(target, there),
            device_id_type=MESH,
        )

    def first_copy(h, j, where):
        return pltpu.make_async_remote_copy(
            src_ref=first_ref.at[where],
            dst_ref=first_ref.at[where],
            send_sem=first_send_sem.at[h, j],
            recv_sem=first_recv_sem.at[j],
            device_id=(h, tile),
            device_id_type=MESH,
        )

    turn = lax.rem(piece_index((1, lanes), 1, piece), per)

    def step(g, _):
        slot = g % DEPTH if isinstance(g, int) else lax.rem(g, DEPTH)
        fetch(g, slot).wait()
        fields = xbuf[slot].reshape(PACK * width, fine)
        across = jnp.dot(zon2[...], fields, preferred_element_type=jnp.float32)
        across_ref[...] = across[lanes:] + across[:lanes]
        for j in range(bands):
            band = lax.rem((1 - side) * (bands // 2) + j, bands)
            first = band * tiles_per_band
            high, middle, low = three_parts(across_ref[:, pl.ds(pl.multiple_of(band * block, block), block)])
            parts = jnp.concatenate([high, middle, low], axis=0)
            out = lax.dot_general(
                mer2[...], parts, (((1,), (1,)), ((), ())), preferred_element_type=jnp.float32
            )
            top, bottom = out[:per_block], out[per_block:]
            total = top[:, 2 * lanes :] + bottom[:, lanes : 2 * lanes]
            total = total + top[:, lanes : 2 * lanes] + bottom[:, :lanes]
            total = total + top[:, :lanes]
            where = pl.ds(pl.multiple_of(band * per_block, per_block), per_block)
            begins = isinstance(g, int)
            if begins:

                @pl.when(me == 0)
                def _():
                    kept = total
                    for m in range(1, per):
                        kept = jnp.where(turn == m, pltpu.roll(total, m * piece, 1), kept)
                    first_ref[where] = kept

                if j == 0:
                    extra = jnp.where(me == 0, members - 1, 0)
                    pl.semaphore_wait(barrier, tiles - jnp.where(stays, 1, 0) + extra)

                @pl.when(me == 0)
                def _():
                    for h in range(1, members):
                        first_copy(h, j, where).start()

                @pl.when(me != 0)
                def _():
                    first_copy(0, j, where).wait_recv()

            total = total - first_ref[where]
            for q in range(tiles_per_band):
                sendbuf[first + q, g] = total[q * rows : (q + 1) * rows]
            if begins and packed:

                @pl.when(me == 0)
                def _():
                    for q in range(tiles_per_band):
                        top = total[q * rows : q * rows + rows // 2]
                        bottom = total[q * rows + rows // 2 : (q + 1) * rows]
                        both = jnp.where(turn == 1, top, pltpu.roll(bottom, lanes - piece, 1))
                        sendbuf[first + q, g, : rows // 2] = both

            for q in range(tiles_per_band):
                there = first + lax.rem(tile + q, tiles_per_band)
                away = None
                if q == 0 and j >= bands // 2:
                    own = stays & (there == tile)
                    away = jnp.logical_not(own)

                    @pl.when(own)
                    def _():
                        pltpu.make_async_copy(sendbuf.at[tile, g], got_ref.at[slot_there, g], own_sem).start()

                if begins and packed:
                    low_end = me == 0 if away is None else (me == 0) & away
                    other = me != 0 if away is None else (me != 0) & away

                    @pl.when(low_end)
                    def _():
                        remote(there, g, True).start()

                    @pl.when(other)
                    def _():
                        remote(there, g).start()

                elif away is not None:

                    @pl.when(away)
                    def _():
                        remote(there, g).start()

                else:
                    remote(there, g).start()

        @pl.when(jnp.asarray(g + DEPTH < groups))
        def _():
            fetch(g + DEPTH, slot).start()

        return 0

    step(0, 0)
    lax.fori_loop(1, groups, step, 0)

    @pl.when(stays)
    def _():
        pltpu.make_async_copy(sendbuf.at[tile], got_ref.at[slot_there], own_sem).wait()

    mean_ref[...] = jnp.zeros_like(mean_ref)

    def arrival(g, _):
        for h in range(members):
            short = packed and isinstance(g, int) and h == 0
            height = rows // 2 if short else rows
            for slot in range(h * spread, (h + 1) * spread):

                @pl.when(jnp.logical_not(stays & (slot_there == slot)))
                def _():
                    pltpu.make_async_remote_copy(
                        src_ref=sendbuf.at[0, g, pl.ds(0, height)],
                        dst_ref=got_ref.at[slot, g, pl.ds(0, height)],
                        send_sem=send_sem.at[0],
                        recv_sem=recv_sem.at[slot, g],
                        device_id=(target, 0),
                        device_id_type=MESH,
                    ).wait_recv()

            for part in range(spread // PACK):
                base = h * spread + part * PACK
                columns = slice(part * lanes, (part + 1) * lanes)
                blocks = [got_ref[base + s, g, :height] for s in range(PACK)]
                if short:
                    blocks = [
                        jnp.concatenate(
                            [jnp.where(turn == 1, both, 0.0), jnp.where(turn == 1, pltpu.roll(both, piece, 1), 0.0)],
                            axis=0,
                        )
                        for both in blocks
                    ]
                fields = swap_pieces(blocks, piece)
                for f in range(PACK):
                    raw_ref[f // per, h * local + g * per + f % per, :, columns] = fields[f]
                for level in range(levels):
                    total = fields[level * per]
                    for m in range(1, per):
                        total = total + fields[level * per + m]
                    mean_ref[level, :, columns] += total
        return 0

    arrival(0, 0)
    lax.fori_loop(1, groups - 1, arrival, 0)
    for there in range(tiles):

        @pl.when(jnp.logical_not(stays & (tile == there)))
        def _():
            rest = pl.ds(1, groups - 1)
            pltpu.make_async_remote_copy(
                src_ref=sendbuf.at[there, rest],
                dst_ref=got_ref.at[slot_there, rest],
                send_sem=send_sem.at[there],
                recv_sem=recv_sem.at[slot_there, 0],
                device_id=(target, there),
                device_id_type=MESH,
            ).wait_send()
            if packed:

                @pl.when(me == 0)
                def _():
                    remote(there, 0, True).wait_send()

                @pl.when(me != 0)
                def _():
                    remote(there, 0).wait_send()

            else:
                remote(there, 0).wait_send()

    @pl.when(me == 0)
    def _():
        for h in range(1, members):
            for j in range(bands):
                first_copy(h, j, pl.ds(j * per_block, per_block)).wait_send()

    lax.fori_loop(groups - 1, groups, arrival, 0)
    mean_ref[...] = mean_ref[...] / count


def center_kernel(chunk, raw_ref, mean_ref, out_ref, outbuf, sem):
    levels, count = raw_ref.shape[:2]
    scale = 1.0 / math.sqrt(count - 1)
    for level in range(levels):
        mean = mean_ref[level]
        for start in range(0, count, chunk):

            def center(m, _, start=start, level=level, mean=mean):
                outbuf[level, start + m] = (raw_ref[level, start + m] - mean) * scale
                return 0

            lax.fori_loop(0, chunk, center, 0, unroll=5)
            at = pl.ds(start, chunk)
            pltpu.make_async_copy(outbuf.at[level, at], out_ref.at[level, at], sem).start()
    pltpu.make_async_copy(outbuf, out_ref, sem).wait()


def body(members, tiles, x, meridional, zonal):
    levels, local, width, fine = x.shape
    block, per_block = meridional.shape
    coarse = zonal.shape[0]
    lanes = PACK * coarse
    groups = levels * local // PACK
    rows = fine // block * per_block // tiles
    spread = tiles // members
    assert PACK % levels == 0 and local % (PACK // levels) == 0 and spread % PACK == 0 and per_block % rows == 0
    assert fine // block % 2 == 0
    anywhere = pl.BlockSpec(memory_space=pl.ANY)
    count = local * members
    columns = spread * coarse
    operators = jnp.concatenate([meridional, jnp.pad(zonal, ((0, 0), (0, per_block - width)))], axis=0)
    raw, mean = pl.pallas_call(
        functools.partial(exchange_kernel, members, tiles, block),
        out_shape=[
            jax.ShapeDtypeStruct((levels, count, rows, columns), jnp.float32),
            jax.ShapeDtypeStruct((levels, rows, columns), jnp.float32),
        ],
        in_specs=[anywhere, pl.BlockSpec(memory_space=pltpu.VMEM)],
        out_specs=[pl.BlockSpec(memory_space=pltpu.VMEM)] * 2,
        scratch_shapes=[
            pltpu.VMEM((DEPTH, levels, PACK // levels, width, fine), jnp.bfloat16),
            pltpu.VMEM((2 * lanes, PACK * width), jnp.bfloat16),
            pltpu.VMEM((2 * per_block, block), jnp.bfloat16),
            pltpu.VMEM((lanes, fine), jnp.float32),
            pltpu.VMEM((tiles, groups, rows, lanes), jnp.float32),
            pltpu.VMEM((tiles, groups, rows, lanes), jnp.float32),
            pltpu.VMEM((tiles * rows, lanes), jnp.float32),
            pltpu.SemaphoreType.DMA((DEPTH,)),
            pltpu.SemaphoreType.DMA((members, fine // block)),
            pltpu.SemaphoreType.DMA((fine // block,)),
            pltpu.SemaphoreType.DMA((tiles,)),
            pltpu.SemaphoreType.DMA((tiles,)),
            pltpu.SemaphoreType.DMA((tiles, groups)),
            pltpu.SemaphoreType.DMA,
        ],
        compiler_params=pltpu.CompilerParams(
            collective_id=0, has_side_effects=True, vmem_limit_bytes=40 * 1024 * 1024
        ),
        name="restrict_exchange",
    )(x, operators)
    return pl.pallas_call(
        functools.partial(center_kernel, 16 if count % 16 == 0 else count),
        out_shape=jax.ShapeDtypeStruct((levels, count, rows, columns), jnp.float32),
        in_specs=[pl.BlockSpec(memory_space=pltpu.VMEM)] * 2,
        out_specs=anywhere,
        scratch_shapes=[
            pltpu.VMEM((levels, count, rows, columns), jnp.float32),
            pltpu.SemaphoreType.DMA,
        ],
        compiler_params=pltpu.CompilerParams(vmem_limit_bytes=16 * 1024 * 1024),
        name="center_scale",
    )(raw, mean)


def solution(mesh):
    members, tiles = mesh.shape["member"], mesh.shape["tile"]
    return jax.shard_map(
        functools.partial(body, members, tiles),
        mesh=mesh,
        in_specs=(P(None, "member", "tile", None), P(), P("tile", None)),
        out_specs=P(None, None, "tile", "member"),
        check_vma=False,
    )
```

```python
import functools
import math

import jax
import jax.numpy as jnp
from jax import lax
from jax.experimental import pallas as pl
from jax.experimental.pallas import tpu as pltpu
from jax.sharding import PartitionSpec as P

MESH = pl.DeviceIdType.MESH
PACK = 8
DEPTH = 3


def two_parts(value):
    high = value.astype(jnp.bfloat16)
    low = (value - high.astype(jnp.float32)).astype(jnp.bfloat16)
    return high, low


def three_parts(value):
    high = value.astype(jnp.bfloat16)
    rest = value - high.astype(jnp.float32)
    middle = rest.astype(jnp.bfloat16)
    low = (rest - middle.astype(jnp.float32)).astype(jnp.bfloat16)
    return high, middle, low


def piece_index(shape, dimension, size):
    at = lax.broadcasted_iota(jnp.int32, shape, dimension)
    piece = jnp.zeros(shape, jnp.int32)
    for f in range(1, PACK):
        piece = piece + jnp.where(at >= f * size, 1, 0)
    return piece


def block_diagonal(part, width):
    coarse = part.shape[0]
    row_piece = piece_index((PACK * coarse, 1), 0, coarse)
    col_piece = piece_index((1, PACK * width), 1, width)
    within = lax.broadcasted_iota(jnp.int32, (1, PACK * width), 1) - col_piece * width
    spread = lax.broadcasted_iota(jnp.int32, (width, PACK * width), 0) == within
    spread = jnp.where(spread, 1.0, 0.0).astype(jnp.bfloat16)
    wide = jnp.dot(part, spread, preferred_element_type=jnp.float32)
    tall = jnp.concatenate([wide] * PACK, axis=0)
    return jnp.where(row_piece == col_piece, tall, 0.0).astype(jnp.bfloat16)


def swap_pieces(blocks, piece):
    lanes = blocks[0].shape[-1]
    lane = lax.broadcasted_iota(jnp.int32, blocks[0].shape, blocks[0].ndim - 1)
    axis = blocks[0].ndim - 1
    blocks = list(blocks)
    d = PACK // 2
    while d >= 1:
        shift = d * piece
        upper = (lane & shift) != 0
        for s in range(PACK):
            if s & d:
                continue
            a, b = blocks[s], blocks[s + d]
            if 2 * shift == lanes:
                both = pltpu.roll(jnp.where(upper, a, b), shift, axis)
                blocks[s] = jnp.where(upper, both, a)
                blocks[s + d] = jnp.where(upper, b, both)
            else:
                blocks[s] = jnp.where(upper, pltpu.roll(b, shift, axis), a)
                blocks[s + d] = jnp.where(upper, b, pltpu.roll(a, lanes - shift, axis))
        d //= 2
    return blocks


def exchange_kernel(
    members,
    tiles,
    block,
    x_ref,
    op_ref,
    raw_ref,
    mean_ref,
    xbuf,
    zon2,
    mer2,
    across_ref,
    sendbuf,
    got_ref,
    first_ref,
    x_sem,
    first_send_sem,
    first_recv_sem,
    short_sem,
    send_sem,
    recv_sem,
    own_sem,
):
    levels, local, width, fine = x_ref.shape
    per_block = op_ref.shape[1]
    groups, rows, lanes = sendbuf.shape[1:]
    per = PACK // levels
    spread = tiles // members
    bands = fine // block
    tiles_per_band = tiles // bands
    count = members * local
    piece = lanes // PACK
    packed = per == 2 and rows % 16 == 0
    me = lax.axis_index("member")
    tile = lax.axis_index("tile")
    target = tile // spread
    slot_there = me * spread + lax.rem(tile, spread)
    stays = target == me
    side = tile // (tiles // 2)
    quarter = tile // (tiles // 4)
    outer = (quarter == 0) | (quarter == 3)
    early = jnp.where(outer, 1 - side, side)

    def fetch(g, slot):
        return pltpu.make_async_copy(x_ref.at[:, pl.ds(g * per, per)], xbuf.at[slot], x_sem.at[slot])

    fetch(0, 0).start()

    barrier = pltpu.get_barrier_semaphore()
    for h in range(members):
        for s in range(spread):
            source = me * spread + s

            @pl.when(jnp.logical_not((h == me) & (source == tile)))
            def _():
                pl.semaphore_signal(barrier, inc=1, device_id=(h, source), device_id_type=MESH)

    @pl.when(me != 0)
    def _():
        pl.semaphore_signal(barrier, inc=1, device_id=(0, tile), device_id_type=MESH)

    zon_high, zon_low = two_parts(op_ref[block : block + piece, :width])
    zon2[:lanes] = block_diagonal(zon_high, width)
    zon2[lanes:] = block_diagonal(zon_low, width)
    mer_high, mer_low = two_parts(op_ref[:block].T)
    mer2[:per_block] = mer_high
    mer2[per_block:] = mer_low
    for g in range(1, min(DEPTH, groups)):
        fetch(g, g).start()

    def remote(there, g, short=False):
        height = pl.ds(0, rows // 2 if short else rows)
        return pltpu.make_async_remote_copy(
            src_ref=sendbuf.at[there, g, height],
            dst_ref=got_ref.at[slot_there, g, height],
            send_sem=(short_sem if isinstance(g, int) else send_sem).at[there],
            recv_sem=recv_sem.at[slot_there, g],
            device_id=(target, there),
            device_id_type=MESH,
        )

    def first_copy(h, j, where):
        return pltpu.make_async_remote_copy(
            src_ref=first_ref.at[where],
            dst_ref=first_ref.at[where],
            send_sem=first_send_sem.at[h, j],
            recv_sem=first_recv_sem.at[j],
            device_id=(h, tile),
            device_id_type=MESH,
        )

    turn = lax.rem(piece_index((1, lanes), 1, piece), per)

    def send(first, g):
        for q in range(tiles_per_band):
            there = first + lax.rem(tile + q, tiles_per_band)
            away = None
            if q == 0:
                own = stays & (there == tile)
                away = jnp.logical_not(own)

                @pl.when(own)
                def _():
                    pltpu.make_async_copy(sendbuf.at[tile, g], got_ref.at[slot_there, g], own_sem).start()

            if isinstance(g, int) and packed:
                low_end = me == 0 if away is None else (me == 0) & away
                other = me != 0 if away is None else (me != 0) & away

                @pl.when(low_end)
                def _():
                    remote(there, g, True).start()

                @pl.when(other)
                def _():
                    remote(there, g).start()

            elif away is not None:

                @pl.when(away)
                def _():
                    remote(there, g).start()

            else:
                remote(there, g).start()

    def step(g, _):
        slot = g % DEPTH if isinstance(g, int) else lax.rem(g, DEPTH)
        fetch(g, slot).wait()
        fields = xbuf[slot].reshape(PACK * width, fine)
        across = jnp.dot(zon2[...], fields, preferred_element_type=jnp.float32)
        across_ref[...] = across[lanes:] + across[:lanes]
        for j in range(bands):
            band = lax.rem(early * (bands // 2) + j, bands)
            first = band * tiles_per_band
            high, middle, low = three_parts(across_ref[:, pl.ds(pl.multiple_of(band * block, block), block)])
            parts = jnp.concatenate([high, middle, low], axis=0)
            out = lax.dot_general(
                mer2[...], parts, (((1,), (1,)), ((), ())), preferred_element_type=jnp.float32
            )
            top, bottom = out[:per_block], out[per_block:]
            total = top[:, 2 * lanes :] + bottom[:, lanes : 2 * lanes]
            total = total + top[:, lanes : 2 * lanes] + bottom[:, :lanes]
            total = total + top[:, :lanes]
            where = pl.ds(pl.multiple_of(band * per_block, per_block), per_block)
            begins = isinstance(g, int)
            if begins:

                @pl.when(me == 0)
                def _():
                    kept = total
                    for m in range(1, per):
                        kept = jnp.where(turn == m, pltpu.roll(total, m * piece, 1), kept)
                    first_ref[where] = kept

                if j == 0:
                    extra = jnp.where(me == 0, members - 1, 0)
                    pl.semaphore_wait(barrier, tiles - jnp.where(stays, 1, 0) + extra)

                @pl.when(me == 0)
                def _():
                    for h in range(1, members):
                        first_copy(h, j, where).start()

                @pl.when(me != 0)
                def _():
                    first_copy(0, j, where).wait_recv()

            total = total - first_ref[where]
            for q in range(tiles_per_band):
                sendbuf[first + q, g] = total[q * rows : (q + 1) * rows]
            if begins and packed:

                @pl.when(me == 0)
                def _():
                    for q in range(tiles_per_band):
                        top = total[q * rows : q * rows + rows // 2]
                        bottom = total[q * rows + rows // 2 : (q + 1) * rows]
                        both = jnp.where(turn == 1, top, pltpu.roll(bottom, lanes - piece, 1))
                        sendbuf[first + q, g, : rows // 2] = both

            if j < bands // 2:
                send(first, g)

        @pl.when(jnp.asarray(g + DEPTH < groups))
        def _():
            fetch(g + DEPTH, slot).start()

        return 0

    def later(g, _):
        for j in range(bands // 2):
            send(((1 - early) * (bands // 2) + j) * tiles_per_band, g)
        return 0

    step(0, 0)
    lax.fori_loop(1, groups, step, 0)
    later(0, 0)
    lax.fori_loop(1, groups, later, 0)

    @pl.when(stays)
    def _():
        pltpu.make_async_copy(sendbuf.at[tile], got_ref.at[slot_there], own_sem).wait()

    mean_ref[...] = jnp.zeros_like(mean_ref)

    def arrival(g, _):
        for h in range(members):
            short = packed and isinstance(g, int) and h == 0
            height = rows // 2 if short else rows
            for slot in range(h * spread, (h + 1) * spread):

                @pl.when(jnp.logical_not(stays & (slot_there == slot)))
                def _():
                    pltpu.make_async_remote_copy(
                        src_ref=sendbuf.at[0, g, pl.ds(0, height)],
                        dst_ref=got_ref.at[slot, g, pl.ds(0, height)],
                        send_sem=send_sem.at[0],
                        recv_sem=recv_sem.at[slot, g],
                        device_id=(target, 0),
                        device_id_type=MESH,
                    ).wait_recv()

            for part in range(spread // PACK):
                base = h * spread + part * PACK
                columns = slice(part * lanes, (part + 1) * lanes)
                blocks = [got_ref[base + s, g, :height] for s in range(PACK)]
                if short:
                    blocks = [
                        jnp.concatenate(
                            [jnp.where(turn == 1, both, 0.0), jnp.where(turn == 1, pltpu.roll(both, piece, 1), 0.0)],
                            axis=0,
                        )
                        for both in blocks
                    ]
                fields = swap_pieces(blocks, piece)
                for f in range(PACK):
                    raw_ref[f // per, h * local + g * per + f % per, :, columns] = fields[f]
                for level in range(levels):
                    total = fields[level * per]
                    for m in range(1, per):
                        total = total + fields[level * per + m]
                    mean_ref[level, :, columns] += total
        return 0

    arrival(0, 0)
    lax.fori_loop(1, groups - 1, arrival, 0)
    for there in range(tiles):

        @pl.when(jnp.logical_not(stays & (tile == there)))
        def _():
            rest = pl.ds(1, groups - 1)
            pltpu.make_async_remote_copy(
                src_ref=sendbuf.at[there, rest],
                dst_ref=got_ref.at[slot_there, rest],
                send_sem=send_sem.at[there],
                recv_sem=recv_sem.at[slot_there, 0],
                device_id=(target, there),
                device_id_type=MESH,
            ).wait_send()
            if packed:

                @pl.when(me == 0)
                def _():
                    remote(there, 0, True).wait_send()

                @pl.when(me != 0)
                def _():
                    remote(there, 0).wait_send()

            else:
                remote(there, 0).wait_send()

    @pl.when(me == 0)
    def _():
        for h in range(1, members):
            for j in range(bands):
                first_copy(h, j, pl.ds(j * per_block, per_block)).wait_send()

    lax.fori_loop(groups - 1, groups, arrival, 0)
    mean_ref[...] = mean_ref[...] / count


def center_kernel(chunk, raw_ref, mean_ref, out_ref, outbuf, sem):
    levels, count = raw_ref.shape[:2]
    scale = 1.0 / math.sqrt(count - 1)
    for level in range(levels):
        mean = mean_ref[level]
        for start in range(0, count, chunk):

            def center(m, _, start=start, level=level, mean=mean):
                outbuf[level, start + m] = (raw_ref[level, start + m] - mean) * scale
                return 0

            lax.fori_loop(0, chunk, center, 0, unroll=5)
            at = pl.ds(start, chunk)
            pltpu.make_async_copy(outbuf.at[level, at], out_ref.at[level, at], sem).start()
    pltpu.make_async_copy(outbuf, out_ref, sem).wait()


def body(members, tiles, x, meridional, zonal):
    levels, local, width, fine = x.shape
    block, per_block = meridional.shape
    coarse = zonal.shape[0]
    lanes = PACK * coarse
    groups = levels * local // PACK
    rows = fine // block * per_block // tiles
    spread = tiles // members
    assert PACK % levels == 0 and local % (PACK // levels) == 0 and spread % PACK == 0 and per_block % rows == 0
    assert fine // block % 2 == 0 and tiles % 4 == 0
    anywhere = pl.BlockSpec(memory_space=pl.ANY)
    count = local * members
    columns = spread * coarse
    operators = jnp.concatenate([meridional, jnp.pad(zonal, ((0, 0), (0, per_block - width)))], axis=0)
    raw, mean = pl.pallas_call(
        functools.partial(exchange_kernel, members, tiles, block),
        out_shape=[
            jax.ShapeDtypeStruct((levels, count, rows, columns), jnp.float32),
            jax.ShapeDtypeStruct((levels, rows, columns), jnp.float32),
        ],
        in_specs=[anywhere, pl.BlockSpec(memory_space=pltpu.VMEM)],
        out_specs=[pl.BlockSpec(memory_space=pltpu.VMEM)] * 2,
        scratch_shapes=[
            pltpu.VMEM((DEPTH, levels, PACK // levels, width, fine), jnp.bfloat16),
            pltpu.VMEM((2 * lanes, PACK * width), jnp.bfloat16),
            pltpu.VMEM((2 * per_block, block), jnp.bfloat16),
            pltpu.VMEM((lanes, fine), jnp.float32),
            pltpu.VMEM((tiles, groups, rows, lanes), jnp.float32),
            pltpu.VMEM((tiles, groups, rows, lanes), jnp.float32),
            pltpu.VMEM((tiles * rows, lanes), jnp.float32),
            pltpu.SemaphoreType.DMA((DEPTH,)),
            pltpu.SemaphoreType.DMA((members, fine // block)),
            pltpu.SemaphoreType.DMA((fine // block,)),
            pltpu.SemaphoreType.DMA((tiles,)),
            pltpu.SemaphoreType.DMA((tiles,)),
            pltpu.SemaphoreType.DMA((tiles, groups)),
            pltpu.SemaphoreType.DMA,
        ],
        compiler_params=pltpu.CompilerParams(
            collective_id=0, has_side_effects=True, vmem_limit_bytes=40 * 1024 * 1024
        ),
        name="restrict_exchange",
    )(x, operators)
    return pl.pallas_call(
        functools.partial(center_kernel, 16 if count % 16 == 0 else count),
        out_shape=jax.ShapeDtypeStruct((levels, count, rows, columns), jnp.float32),
        in_specs=[pl.BlockSpec(memory_space=pltpu.VMEM)] * 2,
        out_specs=anywhere,
        scratch_shapes=[
            pltpu.VMEM((levels, count, rows, columns), jnp.float32),
            pltpu.SemaphoreType.DMA,
        ],
        compiler_params=pltpu.CompilerParams(vmem_limit_bytes=16 * 1024 * 1024),
        name="center_scale",
    )(raw, mean)


def solution(mesh):
    members, tiles = mesh.shape["member"], mesh.shape["tile"]
    return jax.shard_map(
        functools.partial(body, members, tiles),
        mesh=mesh,
        in_specs=(P(None, "member", "tile", None), P(), P("tile", None)),
        out_specs=P(None, None, "tile", "member"),
        check_vma=False,
    )
```

```python
import functools
import math

import jax
import jax.numpy as jnp
from jax import lax
from jax.experimental import pallas as pl
from jax.experimental.pallas import tpu as pltpu
from jax.sharding import PartitionSpec as P

MESH = pl.DeviceIdType.MESH
PACK = 8
DEPTH = 3


def two_parts(value):
    high = value.astype(jnp.bfloat16)
    low = (value - high.astype(jnp.float32)).astype(jnp.bfloat16)
    return high, low


def three_parts(value):
    high = value.astype(jnp.bfloat16)
    rest = value - high.astype(jnp.float32)
    middle = rest.astype(jnp.bfloat16)
    low = (rest - middle.astype(jnp.float32)).astype(jnp.bfloat16)
    return high, middle, low


def piece_index(shape, dimension, size):
    at = lax.broadcasted_iota(jnp.int32, shape, dimension)
    piece = jnp.zeros(shape, jnp.int32)
    for f in range(1, PACK):
        piece = piece + jnp.where(at >= f * size, 1, 0)
    return piece


def block_diagonal(part, width):
    coarse = part.shape[0]
    row_piece = piece_index((PACK * coarse, 1), 0, coarse)
    col_piece = piece_index((1, PACK * width), 1, width)
    within = lax.broadcasted_iota(jnp.int32, (1, PACK * width), 1) - col_piece * width
    spread = lax.broadcasted_iota(jnp.int32, (width, PACK * width), 0) == within
    spread = jnp.where(spread, 1.0, 0.0).astype(jnp.bfloat16)
    wide = jnp.dot(part, spread, preferred_element_type=jnp.float32)
    tall = jnp.concatenate([wide] * PACK, axis=0)
    return jnp.where(row_piece == col_piece, tall, 0.0).astype(jnp.bfloat16)


def swap_pieces(blocks, piece):
    lanes = blocks[0].shape[-1]
    lane = lax.broadcasted_iota(jnp.int32, blocks[0].shape, blocks[0].ndim - 1)
    axis = blocks[0].ndim - 1
    blocks = list(blocks)
    d = PACK // 2
    while d >= 1:
        shift = d * piece
        upper = (lane & shift) != 0
        for s in range(PACK):
            if s & d:
                continue
            a, b = blocks[s], blocks[s + d]
            if 2 * shift == lanes:
                both = pltpu.roll(jnp.where(upper, a, b), shift, axis)
                blocks[s] = jnp.where(upper, both, a)
                blocks[s + d] = jnp.where(upper, b, both)
            else:
                blocks[s] = jnp.where(upper, pltpu.roll(b, shift, axis), a)
                blocks[s + d] = jnp.where(upper, b, pltpu.roll(a, lanes - shift, axis))
        d //= 2
    return blocks


def exchange_kernel(
    members,
    tiles,
    block,
    x_ref,
    op_ref,
    raw_ref,
    mean_ref,
    xbuf,
    zon2,
    mer2,
    sendbuf,
    got_ref,
    first_ref,
    x_sem,
    first_send_sem,
    first_recv_sem,
    short_sem,
    send_sem,
    recv_sem,
    own_sem,
):
    levels, local, width, fine = x_ref.shape
    per_block = op_ref.shape[1]
    groups, rows, lanes = sendbuf.shape[1:]
    per = PACK // levels
    spread = tiles // members
    bands = fine // block
    tiles_per_band = tiles // bands
    count = members * local
    piece = lanes // PACK
    packed = per == 2 and rows % 16 == 0
    me = lax.axis_index("member")
    tile = lax.axis_index("tile")
    target = tile // spread
    slot_there = me * spread + lax.rem(tile, spread)
    stays = target == me
    side = tile // (tiles // 2)

    def fetch(g, slot):
        return pltpu.make_async_copy(x_ref.at[:, pl.ds(g * per, per)], xbuf.at[slot], x_sem.at[slot])

    fetch(0, 0).start()

    barrier = pltpu.get_barrier_semaphore()
    for h in range(members):
        for s in range(spread):
            source = me * spread + s

            @pl.when(jnp.logical_not((h == me) & (source == tile)))
            def _():
                pl.semaphore_signal(barrier, inc=1, device_id=(h, source), device_id_type=MESH)

    @pl.when(me != 0)
    def _():
        pl.semaphore_signal(barrier, inc=1, device_id=(0, tile), device_id_type=MESH)

    zon_high, zon_low = two_parts(op_ref[block : block + piece, :width])
    zon2[:lanes] = block_diagonal(zon_high, width)
    zon2[lanes:] = block_diagonal(zon_low, width)
    mer_high, mer_low = two_parts(op_ref[:block].T)
    mer2[:per_block] = mer_high
    mer2[per_block:] = mer_low
    for g in range(1, min(DEPTH, groups)):
        fetch(g, g).start()

    def remote(there, g, short=False):
        height = pl.ds(0, rows // 2 if short else rows)
        return pltpu.make_async_remote_copy(
            src_ref=sendbuf.at[there, g, height],
            dst_ref=got_ref.at[slot_there, g, height],
            send_sem=(short_sem if isinstance(g, int) else send_sem).at[there],
            recv_sem=recv_sem.at[slot_there, g],
            device_id=(target, there),
            device_id_type=MESH,
        )

    def first_copy(h, j, where):
        return pltpu.make_async_remote_copy(
            src_ref=first_ref.at[where],
            dst_ref=first_ref.at[where],
            send_sem=first_send_sem.at[h, j],
            recv_sem=first_recv_sem.at[j],
            device_id=(h, tile),
            device_id_type=MESH,
        )

    turn = lax.rem(piece_index((1, lanes), 1, piece), per)

    def step(g, _):
        slot = g % DEPTH if isinstance(g, int) else lax.rem(g, DEPTH)
        fetch(g, slot).wait()
        for j in range(bands):
            band = lax.rem((1 - side) * (bands // 2) + j, bands)
            first = band * tiles_per_band
            latitudes = pl.ds(pl.multiple_of(band * block, block), block)
            fields = xbuf[slot, :, :, :, latitudes].reshape(PACK * width, block)
            across = jnp.dot(zon2[...], fields, preferred_element_type=jnp.float32)
            high, middle, low = three_parts(across[lanes:] + across[:lanes])
            parts = jnp.concatenate([high, middle, low], axis=0)
            out = lax.dot_general(
                mer2[...], parts, (((1,), (1,)), ((), ())), preferred_element_type=jnp.float32
            )
            top, bottom = out[:per_block], out[per_block:]
            total = top[:, 2 * lanes :] + bottom[:, lanes : 2 * lanes]
            total = total + top[:, lanes : 2 * lanes] + bottom[:, :lanes]
            total = total + top[:, :lanes]
            where = pl.ds(pl.multiple_of(band * per_block, per_block), per_block)
            begins = isinstance(g, int)
            if begins:

                @pl.when(me == 0)
                def _():
                    kept = total
                    for m in range(1, per):
                        kept = jnp.where(turn == m, pltpu.roll(total, m * piece, 1), kept)
                    first_ref[where] = kept

                if j == 0:
                    extra = jnp.where(me == 0, members - 1, 0)
                    pl.semaphore_wait(barrier, tiles - jnp.where(stays, 1, 0) + extra)

                @pl.when(me == 0)
                def _():
                    for h in range(1, members):
                        first_copy(h, j, where).start()

                @pl.when(me != 0)
                def _():
                    first_copy(0, j, where).wait_recv()

            total = total - first_ref[where]
            for q in range(tiles_per_band):
                sendbuf[first + q, g] = total[q * rows : (q + 1) * rows]
            if begins and packed:

                @pl.when(me == 0)
                def _():
                    for q in range(tiles_per_band):
                        top = total[q * rows : q * rows + rows // 2]
                        bottom = total[q * rows + rows // 2 : (q + 1) * rows]
                        both = jnp.where(turn == 1, top, pltpu.roll(bottom, lanes - piece, 1))
                        sendbuf[first + q, g, : rows // 2] = both

            for q in range(tiles_per_band):
                there = first + lax.rem(tile + q, tiles_per_band)
                away = None
                if q == 0 and j >= bands // 2:
                    own = stays & (there == tile)
                    away = jnp.logical_not(own)

                    @pl.when(own)
                    def _():
                        pltpu.make_async_copy(sendbuf.at[tile, g], got_ref.at[slot_there, g], own_sem).start()

                if begins and packed:
                    low_end = me == 0 if away is None else (me == 0) & away
                    other = me != 0 if away is None else (me != 0) & away

                    @pl.when(low_end)
                    def _():
                        remote(there, g, True).start()

                    @pl.when(other)
                    def _():
                        remote(there, g).start()

                elif away is not None:

                    @pl.when(away)
                    def _():
                        remote(there, g).start()

                else:
                    remote(there, g).start()

        @pl.when(jnp.asarray(g + DEPTH < groups))
        def _():
            fetch(g + DEPTH, slot).start()

        return 0

    step(0, 0)
    lax.fori_loop(1, groups, step, 0)

    @pl.when(stays)
    def _():
        pltpu.make_async_copy(sendbuf.at[tile], got_ref.at[slot_there], own_sem).wait()

    mean_ref[...] = jnp.zeros_like(mean_ref)

    def arrival(g, _):
        for h in range(members):
            short = packed and isinstance(g, int) and h == 0
            height = rows // 2 if short else rows
            for slot in range(h * spread, (h + 1) * spread):

                @pl.when(jnp.logical_not(stays & (slot_there == slot)))
                def _():
                    pltpu.make_async_remote_copy(
                        src_ref=sendbuf.at[0, g, pl.ds(0, height)],
                        dst_ref=got_ref.at[slot, g, pl.ds(0, height)],
                        send_sem=send_sem.at[0],
                        recv_sem=recv_sem.at[slot, g],
                        device_id=(target, 0),
                        device_id_type=MESH,
                    ).wait_recv()

            for part in range(spread // PACK):
                base = h * spread + part * PACK
                columns = slice(part * lanes, (part + 1) * lanes)
                blocks = [got_ref[base + s, g, :height] for s in range(PACK)]
                if short:
                    blocks = [
                        jnp.concatenate(
                            [jnp.where(turn == 1, both, 0.0), jnp.where(turn == 1, pltpu.roll(both, piece, 1), 0.0)],
                            axis=0,
                        )
                        for both in blocks
                    ]
                fields = swap_pieces(blocks, piece)
                for f in range(PACK):
                    raw_ref[f // per, h * local + g * per + f % per, :, columns] = fields[f]
                for level in range(levels):
                    total = fields[level * per]
                    for m in range(1, per):
                        total = total + fields[level * per + m]
                    mean_ref[level, :, columns] += total
        return 0

    arrival(0, 0)
    lax.fori_loop(1, groups - 1, arrival, 0)
    for there in range(tiles):

        @pl.when(jnp.logical_not(stays & (tile == there)))
        def _():
            rest = pl.ds(1, groups - 1)
            pltpu.make_async_remote_copy(
                src_ref=sendbuf.at[there, rest],
                dst_ref=got_ref.at[slot_there, rest],
                send_sem=send_sem.at[there],
                recv_sem=recv_sem.at[slot_there, 0],
                device_id=(target, there),
                device_id_type=MESH,
            ).wait_send()
            if packed:

                @pl.when(me == 0)
                def _():
                    remote(there, 0, True).wait_send()

                @pl.when(me != 0)
                def _():
                    remote(there, 0).wait_send()

            else:
                remote(there, 0).wait_send()

    @pl.when(me == 0)
    def _():
        for h in range(1, members):
            for j in range(bands):
                first_copy(h, j, pl.ds(j * per_block, per_block)).wait_send()

    lax.fori_loop(groups - 1, groups, arrival, 0)
    mean_ref[...] = mean_ref[...] / count


def center_kernel(chunk, raw_ref, mean_ref, out_ref, outbuf, sem):
    levels, count = raw_ref.shape[:2]
    scale = 1.0 / math.sqrt(count - 1)
    for level in range(levels):
        mean = mean_ref[level]
        for start in range(0, count, chunk):

            def center(m, _, start=start, level=level, mean=mean):
                outbuf[level, start + m] = (raw_ref[level, start + m] - mean) * scale
                return 0

            lax.fori_loop(0, chunk, center, 0, unroll=5)
            at = pl.ds(start, chunk)
            pltpu.make_async_copy(outbuf.at[level, at], out_ref.at[level, at], sem).start()
    pltpu.make_async_copy(outbuf, out_ref, sem).wait()


def body(members, tiles, x, meridional, zonal):
    levels, local, width, fine = x.shape
    block, per_block = meridional.shape
    coarse = zonal.shape[0]
    lanes = PACK * coarse
    groups = levels * local // PACK
    rows = fine // block * per_block // tiles
    spread = tiles // members
    assert PACK % levels == 0 and local % (PACK // levels) == 0 and spread % PACK == 0 and per_block % rows == 0
    assert fine // block % 2 == 0
    anywhere = pl.BlockSpec(memory_space=pl.ANY)
    count = local * members
    columns = spread * coarse
    operators = jnp.concatenate([meridional, jnp.pad(zonal, ((0, 0), (0, per_block - width)))], axis=0)
    raw, mean = pl.pallas_call(
        functools.partial(exchange_kernel, members, tiles, block),
        out_shape=[
            jax.ShapeDtypeStruct((levels, count, rows, columns), jnp.float32),
            jax.ShapeDtypeStruct((levels, rows, columns), jnp.float32),
        ],
        in_specs=[anywhere, pl.BlockSpec(memory_space=pltpu.VMEM)],
        out_specs=[pl.BlockSpec(memory_space=pltpu.VMEM)] * 2,
        scratch_shapes=[
            pltpu.VMEM((DEPTH, levels, PACK // levels, width, fine), jnp.bfloat16),
            pltpu.VMEM((2 * lanes, PACK * width), jnp.bfloat16),
            pltpu.VMEM((2 * per_block, block), jnp.bfloat16),
            pltpu.VMEM((tiles, groups, rows, lanes), jnp.float32),
            pltpu.VMEM((tiles, groups, rows, lanes), jnp.float32),
            pltpu.VMEM((tiles * rows, lanes), jnp.float32),
            pltpu.SemaphoreType.DMA((DEPTH,)),
            pltpu.SemaphoreType.DMA((members, fine // block)),
            pltpu.SemaphoreType.DMA((fine // block,)),
            pltpu.SemaphoreType.DMA((tiles,)),
            pltpu.SemaphoreType.DMA((tiles,)),
            pltpu.SemaphoreType.DMA((tiles, groups)),
            pltpu.SemaphoreType.DMA,
        ],
        compiler_params=pltpu.CompilerParams(
            collective_id=0, has_side_effects=True, vmem_limit_bytes=40 * 1024 * 1024
        ),
        name="restrict_exchange",
    )(x, operators)
    return pl.pallas_call(
        functools.partial(center_kernel, 16 if count % 16 == 0 else count),
        out_shape=jax.ShapeDtypeStruct((levels, count, rows, columns), jnp.float32),
        in_specs=[pl.BlockSpec(memory_space=pltpu.VMEM)] * 2,
        out_specs=anywhere,
        scratch_shapes=[
            pltpu.VMEM((levels, count, rows, columns), jnp.float32),
            pltpu.SemaphoreType.DMA,
        ],
        compiler_params=pltpu.CompilerParams(vmem_limit_bytes=16 * 1024 * 1024),
        name="center_scale",
    )(raw, mean)


def solution(mesh):
    members, tiles = mesh.shape["member"], mesh.shape["tile"]
    return jax.shard_map(
        functools.partial(body, members, tiles),
        mesh=mesh,
        in_specs=(P(None, "member", "tile", None), P(), P("tile", None)),
        out_specs=P(None, None, "tile", "member"),
        check_vma=False,
    )
```

```python
import functools
import math

import jax
import jax.numpy as jnp
from jax import lax
from jax.experimental import pallas as pl
from jax.experimental.pallas import tpu as pltpu
from jax.sharding import PartitionSpec as P

MESH = pl.DeviceIdType.MESH
PACK = 8
DEPTH = 3


def two_parts(value):
    high = value.astype(jnp.bfloat16)
    low = (value - high.astype(jnp.float32)).astype(jnp.bfloat16)
    return high, low


def three_parts(value):
    high = value.astype(jnp.bfloat16)
    rest = value - high.astype(jnp.float32)
    middle = rest.astype(jnp.bfloat16)
    low = (rest - middle.astype(jnp.float32)).astype(jnp.bfloat16)
    return high, middle, low


def piece_index(shape, dimension, size):
    at = lax.broadcasted_iota(jnp.int32, shape, dimension)
    piece = jnp.zeros(shape, jnp.int32)
    for f in range(1, PACK):
        piece = piece + jnp.where(at >= f * size, 1, 0)
    return piece


def block_diagonal(part, width):
    coarse = part.shape[0]
    row_piece = piece_index((PACK * coarse, 1), 0, coarse)
    col_piece = piece_index((1, PACK * width), 1, width)
    within = lax.broadcasted_iota(jnp.int32, (1, PACK * width), 1) - col_piece * width
    spread = lax.broadcasted_iota(jnp.int32, (width, PACK * width), 0) == within
    spread = jnp.where(spread, 1.0, 0.0).astype(jnp.bfloat16)
    wide = jnp.dot(part, spread, preferred_element_type=jnp.float32)
    tall = jnp.concatenate([wide] * PACK, axis=0)
    return jnp.where(row_piece == col_piece, tall, 0.0).astype(jnp.bfloat16)


def swap_pieces(blocks, piece):
    lanes = blocks[0].shape[-1]
    lane = lax.broadcasted_iota(jnp.int32, blocks[0].shape, blocks[0].ndim - 1)
    axis = blocks[0].ndim - 1
    blocks = list(blocks)
    d = PACK // 2
    while d >= 1:
        shift = d * piece
        upper = (lane & shift) != 0
        for s in range(PACK):
            if s & d:
                continue
            a, b = blocks[s], blocks[s + d]
            if 2 * shift == lanes:
                both = pltpu.roll(jnp.where(upper, a, b), shift, axis)
                blocks[s] = jnp.where(upper, both, a)
                blocks[s + d] = jnp.where(upper, b, both)
            else:
                blocks[s] = jnp.where(upper, pltpu.roll(b, shift, axis), a)
                blocks[s + d] = jnp.where(upper, b, pltpu.roll(a, lanes - shift, axis))
        d //= 2
    return blocks


def exchange_kernel(
    members,
    tiles,
    block,
    x_ref,
    op_ref,
    raw_ref,
    mean_ref,
    xbuf,
    zon2,
    mer2,
    sendbuf,
    got_ref,
    first_ref,
    x_sem,
    first_send_sem,
    first_recv_sem,
    short_sem,
    send_sem,
    recv_sem,
    own_sem,
):
    levels, local, width, fine = x_ref.shape
    per_block = op_ref.shape[1]
    groups, rows, lanes = sendbuf.shape[1:]
    per = PACK // levels
    spread = tiles // members
    bands = fine // block
    tiles_per_band = tiles // bands
    count = members * local
    piece = lanes // PACK
    packed = per == 2 and rows % 16 == 0
    me = lax.axis_index("member")
    tile = lax.axis_index("tile")
    target = tile // spread
    slot_there = me * spread + lax.rem(tile, spread)
    stays = target == me
    side = tile // (tiles // 2)

    def fetch(g, slot):
        return pltpu.make_async_copy(x_ref.at[:, pl.ds(g * per, per)], xbuf.at[slot], x_sem.at[slot])

    fetch(0, 0).start()

    barrier = pltpu.get_barrier_semaphore()
    for h in range(members):
        for s in range(spread):
            source = me * spread + s

            @pl.when(jnp.logical_not((h == me) & (source == tile)))
            def _():
                pl.semaphore_signal(barrier, inc=1, device_id=(h, source), device_id_type=MESH)

    @pl.when(me != 0)
    def _():
        pl.semaphore_signal(barrier, inc=1, device_id=(0, tile), device_id_type=MESH)

    zon_high, zon_low = two_parts(op_ref[block : block + piece, :width])
    zon2[:lanes] = block_diagonal(zon_high, width)
    zon2[lanes:] = block_diagonal(zon_low, width)
    mer_high, mer_low = two_parts(op_ref[:block].T)
    mer2[:per_block] = mer_high
    mer2[per_block:] = mer_low
    for g in range(1, min(DEPTH, groups)):
        fetch(g, g).start()

    def remote(there, g, short=False):
        height = pl.ds(0, rows // 2 if short else rows)
        return pltpu.make_async_remote_copy(
            src_ref=sendbuf.at[there, g, height],
            dst_ref=got_ref.at[slot_there, g, height],
            send_sem=(short_sem if isinstance(g, int) else send_sem).at[there],
            recv_sem=recv_sem.at[slot_there, g],
            device_id=(target, there),
            device_id_type=MESH,
        )

    def first_copy(h, j, where):
        return pltpu.make_async_remote_copy(
            src_ref=first_ref.at[where],
            dst_ref=first_ref.at[where],
            send_sem=first_send_sem.at[h, j],
            recv_sem=first_recv_sem.at[j],
            device_id=(h, tile),
            device_id_type=MESH,
        )

    turn = lax.rem(piece_index((1, lanes), 1, piece), per)

    def send(first, span, g):
        for q in range(span):
            there = first + lax.rem(tile + q, span)
            away = None
            if q == 0:
                own = stays & (there == tile)
                away = jnp.logical_not(own)

                @pl.when(own)
                def _():
                    pltpu.make_async_copy(sendbuf.at[tile, g], got_ref.at[slot_there, g], own_sem).start()

            if isinstance(g, int) and packed:
                low_end = me == 0 if away is None else (me == 0) & away
                other = me != 0 if away is None else (me != 0) & away

                @pl.when(low_end)
                def _():
                    remote(there, g, True).start()

                @pl.when(other)
                def _():
                    remote(there, g).start()

            elif away is not None:

                @pl.when(away)
                def _():
                    remote(there, g).start()

            else:
                remote(there, g).start()

    def step(g, _):
        slot = g % DEPTH if isinstance(g, int) else lax.rem(g, DEPTH)
        fetch(g, slot).wait()
        for j in range(bands):
            band = lax.rem((1 - side) * (bands // 2) + j, bands)
            first = band * tiles_per_band
            latitudes = pl.ds(pl.multiple_of(band * block, block), block)
            fields = xbuf[slot, :, :, :, latitudes].reshape(PACK * width, block)
            across = jnp.dot(zon2[...], fields, preferred_element_type=jnp.float32)
            high, middle, low = three_parts(across[lanes:] + across[:lanes])
            parts = jnp.concatenate([high, middle, low], axis=0)
            out = lax.dot_general(
                mer2[...], parts, (((1,), (1,)), ((), ())), preferred_element_type=jnp.float32
            )
            top, bottom = out[:per_block], out[per_block:]
            total = top[:, 2 * lanes :] + bottom[:, lanes : 2 * lanes]
            total = total + top[:, lanes : 2 * lanes] + bottom[:, :lanes]
            total = total + top[:, :lanes]
            where = pl.ds(pl.multiple_of(band * per_block, per_block), per_block)
            begins = isinstance(g, int)
            if begins:

                @pl.when(me == 0)
                def _():
                    kept = total
                    for m in range(1, per):
                        kept = jnp.where(turn == m, pltpu.roll(total, m * piece, 1), kept)
                    first_ref[where] = kept

                if j == 0:
                    extra = jnp.where(me == 0, members - 1, 0)
                    pl.semaphore_wait(barrier, tiles - jnp.where(stays, 1, 0) + extra)

                @pl.when(me == 0)
                def _():
                    for h in range(1, members):
                        first_copy(h, j, where).start()

                @pl.when(me != 0)
                def _():
                    first_copy(0, j, where).wait_recv()

            total = total - first_ref[where]
            for q in range(tiles_per_band):
                sendbuf[first + q, g] = total[q * rows : (q + 1) * rows]
            if begins and packed:

                @pl.when(me == 0)
                def _():
                    for q in range(tiles_per_band):
                        top = total[q * rows : q * rows + rows // 2]
                        bottom = total[q * rows + rows // 2 : (q + 1) * rows]
                        both = jnp.where(turn == 1, top, pltpu.roll(bottom, lanes - piece, 1))
                        sendbuf[first + q, g, : rows // 2] = both

            if begins:
                send(first, tiles_per_band, g)
            elif (j + 1) % (bands // 2) == 0:
                far = 1 - side if j < bands // 2 else side
                send(far * (tiles // 2), tiles // 2, g)

        @pl.when(jnp.asarray(g + DEPTH < groups))
        def _():
            fetch(g + DEPTH, slot).start()

        return 0

    step(0, 0)
    lax.fori_loop(1, groups, step, 0)

    @pl.when(stays)
    def _():
        pltpu.make_async_copy(sendbuf.at[tile], got_ref.at[slot_there], own_sem).wait()

    mean_ref[...] = jnp.zeros_like(mean_ref)

    def arrival(g, _):
        for h in range(members):
            short = packed and isinstance(g, int) and h == 0
            height = rows // 2 if short else rows
            for slot in range(h * spread, (h + 1) * spread):

                @pl.when(jnp.logical_not(stays & (slot_there == slot)))
                def _():
                    pltpu.make_async_remote_copy(
                        src_ref=sendbuf.at[0, g, pl.ds(0, height)],
                        dst_ref=got_ref.at[slot, g, pl.ds(0, height)],
                        send_sem=send_sem.at[0],
                        recv_sem=recv_sem.at[slot, g],
                        device_id=(target, 0),
                        device_id_type=MESH,
                    ).wait_recv()

            for part in range(spread // PACK):
                base = h * spread + part * PACK
                columns = slice(part * lanes, (part + 1) * lanes)
                blocks = [got_ref[base + s, g, :height] for s in range(PACK)]
                if short:
                    blocks = [
                        jnp.concatenate(
                            [jnp.where(turn == 1, both, 0.0), jnp.where(turn == 1, pltpu.roll(both, piece, 1), 0.0)],
                            axis=0,
                        )
                        for both in blocks
                    ]
                fields = swap_pieces(blocks, piece)
                for f in range(PACK):
                    raw_ref[f // per, h * local + g * per + f % per, :, columns] = fields[f]
                for level in range(levels):
                    total = fields[level * per]
                    for m in range(1, per):
                        total = total + fields[level * per + m]
                    mean_ref[level, :, columns] += total
        return 0

    arrival(0, 0)
    lax.fori_loop(1, groups - 1, arrival, 0)
    for there in range(tiles):

        @pl.when(jnp.logical_not(stays & (tile == there)))
        def _():
            rest = pl.ds(1, groups - 1)
            pltpu.make_async_remote_copy(
                src_ref=sendbuf.at[there, rest],
                dst_ref=got_ref.at[slot_there, rest],
                send_sem=send_sem.at[there],
                recv_sem=recv_sem.at[slot_there, 0],
                device_id=(target, there),
                device_id_type=MESH,
            ).wait_send()
            if packed:

                @pl.when(me == 0)
                def _():
                    remote(there, 0, True).wait_send()

                @pl.when(me != 0)
                def _():
                    remote(there, 0).wait_send()

            else:
                remote(there, 0).wait_send()

    @pl.when(me == 0)
    def _():
        for h in range(1, members):
            for j in range(bands):
                first_copy(h, j, pl.ds(j * per_block, per_block)).wait_send()

    lax.fori_loop(groups - 1, groups, arrival, 0)
    mean_ref[...] = mean_ref[...] / count


def center_kernel(chunk, raw_ref, mean_ref, out_ref, outbuf, sem):
    levels, count = raw_ref.shape[:2]
    scale = 1.0 / math.sqrt(count - 1)
    for level in range(levels):
        mean = mean_ref[level]
        for start in range(0, count, chunk):

            def center(m, _, start=start, level=level, mean=mean):
                outbuf[level, start + m] = (raw_ref[level, start + m] - mean) * scale
                return 0

            lax.fori_loop(0, chunk, center, 0, unroll=5)
            at = pl.ds(start, chunk)
            pltpu.make_async_copy(outbuf.at[level, at], out_ref.at[level, at], sem).start()
    pltpu.make_async_copy(outbuf, out_ref, sem).wait()


def body(members, tiles, x, meridional, zonal):
    levels, local, width, fine = x.shape
    block, per_block = meridional.shape
    coarse = zonal.shape[0]
    lanes = PACK * coarse
    groups = levels * local // PACK
    rows = fine // block * per_block // tiles
    spread = tiles // members
    assert PACK % levels == 0 and local % (PACK // levels) == 0 and spread % PACK == 0 and per_block % rows == 0
    assert fine // block % 2 == 0
    anywhere = pl.BlockSpec(memory_space=pl.ANY)
    count = local * members
    columns = spread * coarse
    operators = jnp.concatenate([meridional, jnp.pad(zonal, ((0, 0), (0, per_block - width)))], axis=0)
    raw, mean = pl.pallas_call(
        functools.partial(exchange_kernel, members, tiles, block),
        out_shape=[
            jax.ShapeDtypeStruct((levels, count, rows, columns), jnp.float32),
            jax.ShapeDtypeStruct((levels, rows, columns), jnp.float32),
        ],
        in_specs=[anywhere, pl.BlockSpec(memory_space=pltpu.VMEM)],
        out_specs=[pl.BlockSpec(memory_space=pltpu.VMEM)] * 2,
        scratch_shapes=[
            pltpu.VMEM((DEPTH, levels, PACK // levels, width, fine), jnp.bfloat16),
            pltpu.VMEM((2 * lanes, PACK * width), jnp.bfloat16),
            pltpu.VMEM((2 * per_block, block), jnp.bfloat16),
            pltpu.VMEM((tiles, groups, rows, lanes), jnp.float32),
            pltpu.VMEM((tiles, groups, rows, lanes), jnp.float32),
            pltpu.VMEM((tiles * rows, lanes), jnp.float32),
            pltpu.SemaphoreType.DMA((DEPTH,)),
            pltpu.SemaphoreType.DMA((members, fine // block)),
            pltpu.SemaphoreType.DMA((fine // block,)),
            pltpu.SemaphoreType.DMA((tiles,)),
            pltpu.SemaphoreType.DMA((tiles,)),
            pltpu.SemaphoreType.DMA((tiles, groups)),
            pltpu.SemaphoreType.DMA,
        ],
        compiler_params=pltpu.CompilerParams(
            collective_id=0, has_side_effects=True, vmem_limit_bytes=40 * 1024 * 1024
        ),
        name="restrict_exchange",
    )(x, operators)
    return pl.pallas_call(
        functools.partial(center_kernel, 16 if count % 16 == 0 else count),
        out_shape=jax.ShapeDtypeStruct((levels, count, rows, columns), jnp.float32),
        in_specs=[pl.BlockSpec(memory_space=pltpu.VMEM)] * 2,
        out_specs=anywhere,
        scratch_shapes=[
            pltpu.VMEM((levels, count, rows, columns), jnp.float32),
            pltpu.SemaphoreType.DMA,
        ],
        compiler_params=pltpu.CompilerParams(vmem_limit_bytes=16 * 1024 * 1024),
        name="center_scale",
    )(raw, mean)


def solution(mesh):
    members, tiles = mesh.shape["member"], mesh.shape["tile"]
    return jax.shard_map(
        functools.partial(body, members, tiles),
        mesh=mesh,
        in_specs=(P(None, "member", "tile", None), P(), P("tile", None)),
        out_specs=P(None, None, "tile", "member"),
        check_vma=False,
    )
```
